128 devices in a mesh: row: 8 (over z, x_hi), col: 16 (over x_lo, y, core).
Axes of the slice: x: 4 (x_hi: 2, x_lo: 2; x = x_hi * 2 + x_lo), y: 4, z: 4, core: 2. Of those that a mesh axis runs over, the one named last changes fastest.
Arguments:
- rects: int32 [4, 65536], P(None, ('row', 'col')), may hold values from 0 to 2048, as said below
- owner: int32 [65536], P(('row', 'col')), may hold values from 0 to 127, as said below
- counts: int32 [128], P(('row', 'col')), may hold values from 256 to 512
- target: int32 [1024, 8192], P('row', 'col'), may hold values 0 or 1
- loss_weight: float32 [1024, 8192], P('row', 'col'), may hold values from 0.03 to 30, as said below
- kernel: bfloat16 [8, 33, 33], replicated, may hold values from -0.1875 to 0.1875
- socs_weight: float32 [4], replicated, may hold values from 0.25 to 1
Outputs:
- mask_grad: float32 [1024, 8192], P('row', 'col')
- loss: float32 [1], replicated
The draws below stay inside these ranges and needn't reach their ends.
Inputs may be any that keep to these rules, and one draw needn't show every extreme that they name: `owner`: tiles are numbered row index times 16 plus col index. Among the live slots of one layout partition, no tile is named more than 8 times; some tile is named exactly 8 times by the live slots of every partition. Dead slots hold arbitrary tiles. `rects`: every slot has x_lo < x_hi <= 2048, y_lo < y_hi <= 512, x_hi - x_lo at most 64 and y_hi - y_lo at most 48. `loss_weight`: Positive.
All inputs are finite; a program needn't handle non-finite values. No bound on the sum of `target` on one device may be relied on, other than what follows from the above.
Results may differ from the reference program's by a relative error of at most 0.0027.
Values may be sent and summed in bfloat16 or wider, within the bound.
No kernel may reach another device: no remote copies, remote signals or barrier semaphores. Data moves between devices by JAX's collectives and lax.ppermute only.
A program may use at most 64 MiB of HBM per device.

```python
import math
import jax
import jax.numpy as jnp
from jax import lax

TR = 128
TC = 512
RAD = 16
NK = 4
CAP = 8
KS = 33
RECT_DEV = 512
H = 1024
W = 8192
N_COL = 16
DEVICES = 128


def one_order(order_key):
    return jax.random.permutation(order_key, DEVICES - 1)


def partition_routes(key):
    subkeys = jax.random.split(key, 6)
    hot_tile = jax.random.randint(subkeys[0], (), 0, DEVICES)
    fullest = jax.random.randint(subkeys[1], (), 0, DEVICES)
    source_ids = jnp.arange(DEVICES, dtype=jnp.int32)
    live_counts = jax.random.randint(subkeys[2], (DEVICES,), RECT_DEV // 2, RECT_DEV + 1)
    live_counts = jnp.where(source_ids == fullest, RECT_DEV, live_counts).astype(jnp.int32)
    block_sizes = jax.random.randint(subkeys[3], (DEVICES, DEVICES - 1), CAP // 2, CAP + 1).astype(jnp.int32)
    block_sizes = jnp.concatenate([jnp.full((DEVICES, 1), CAP, jnp.int32), block_sizes], axis=1)
    block_starts = jnp.cumsum(block_sizes, axis=1) - block_sizes
    slot_ids = jnp.arange(RECT_DEV, dtype=jnp.int32)
    position = jnp.sum((slot_ids[None, :, None] >= block_starts[:, None, :]).astype(jnp.int32), axis=2) - 1
    orders = jax.vmap(one_order)(jax.random.split(subkeys[4], DEVICES)).astype(jnp.int32)
    chosen = jnp.take_along_axis(orders, jnp.maximum(position - 1, 0), axis=1)
    targets = jnp.where(position == 0, hot_tile, (hot_tile + 1 + chosen) % DEVICES)
    filler = jax.random.randint(subkeys[5], (DEVICES, RECT_DEV), 0, DEVICES)
    owners = jnp.where(slot_ids[None, :] < live_counts[:, None], targets, filler)
    return (owners.reshape(-1).astype(jnp.int32), live_counts)


def draw_owner(key, part):
    return partition_routes(key)[0]


def draw_counts(key, part):
    return partition_routes(key)[1]


def draw_rects(key, part):
    key = jax.random.fold_in(key, 7)
    subkeys = jax.random.split(key, 4)
    total_slots = RECT_DEV * DEVICES
    left_edge = jax.random.randint(subkeys[0], (total_slots,), 0, 4 * TC - 64 + 1)
    across = jax.random.randint(subkeys[1], (total_slots,), 4, 65)
    bottom_edge = jax.random.randint(subkeys[2], (total_slots,), 0, 4 * TR - 48 + 1)
    height = jax.random.randint(subkeys[3], (total_slots,), 4, 49)
    table = jnp.stack([left_edge, left_edge + across, bottom_edge, bottom_edge + height]).astype(jnp.int32)
    table = table.at[:, 0].set(jnp.array([4 * TC - 64, 4 * TC, 4 * TR - 48, 4 * TR], jnp.int32))
    table = table.at[:, 1].set(jnp.array([0, 4, 0, 4], jnp.int32))
    return table


def draw_loss_weight(key, part):
    key = jax.random.fold_in(key, 11)
    row_frac = (jnp.arange(H, dtype=jnp.float32) / H)[:, None]
    col_frac = (jnp.arange(W, dtype=jnp.float32) / W)[None, :]
    spread = jax.random.uniform(key, (H, W), jnp.float32)
    return 10.0 ** (spread - 0.5) * 3.0 ** (row_frac + col_frac - 1.0)


def set_ends(values, stream_key, smallest, largest):
    shape = values.shape
    spot = [jax.random.randint(jax.random.fold_in(stream_key, axis), (), 0, shape[axis]) for axis in range(len(shape))]
    values = values.at[tuple(spot)].set(smallest)
    longest = shape.index(max(shape))
    spot[longest] = (spot[longest] + 1) % shape[longest]
    return values.at[tuple(spot)].set(largest)


def noise(key, shape, deviation, limit, kind=jnp.bfloat16):
    result = jax.random.normal(key, shape, jnp.float32) * deviation
    return jnp.minimum(jnp.maximum(result, -limit), limit).astype(kind)


def setup_inputs(seed: int = 0) -> dict:
    key_list = jax.random.split(jax.random.key(seed), 8)
    rects = draw_rects(jax.random.fold_in(key_list[7], 71), 0)
    owner = draw_owner(jax.random.fold_in(key_list[7], 71), 0)
    counts = draw_counts(jax.random.fold_in(key_list[7], 71), 0)
    target = set_ends((jax.random.randint(key_list[3], (H, W), 0, 2) < 1).astype(jnp.int32), jax.random.fold_in(key_list[3], 1), 0, 1)
    loss_weight = draw_loss_weight(jax.random.fold_in(key_list[7], 71), 0)
    kernel = noise(key_list[5], (2 * NK, KS, KS), (KS * KS) ** -0.5, 0.1875)
    socs_weight = jnp.clip(jnp.exp(jax.random.uniform(key_list[6], (NK,), jnp.float32, math.log(0.25), math.log(1.0))), 0.25, 1.0)
    return dict(rects=rects, owner=owner, counts=counts, target=target, loss_weight=loss_weight, kernel=kernel, socs_weight=socs_weight)


def cover_cells(lower_edge, upper_edge, first_cell, cell_count):
    cell_ids = first_cell[:, None] + jnp.arange(cell_count, dtype=jnp.int32)[None, :]
    cell_edges = 4.0 * cell_ids.astype(jnp.float32)
    spans = jnp.minimum(upper_edge[:, None], cell_edges + 4.0) - jnp.maximum(lower_edge[:, None], cell_edges)
    return jnp.clip(spans, 0.0, 4.0) / 4.0


def reference(rects, owner, counts, target, loss_weight, kernel, socs_weight):
    slot_ids = jnp.arange(RECT_DEV * DEVICES, dtype=jnp.int32)
    live = ((slot_ids % RECT_DEV) < counts[slot_ids // RECT_DEV]).astype(jnp.float32)
    coords = rects.astype(jnp.float32)
    first_row = rects[2] // 4
    first_col = rects[0] // 4
    row_cover = cover_cells(coords[2], coords[3], first_row, 16) * live[:, None]
    col_cover = cover_cells(coords[0], coords[1], first_col, 24)
    rows_at = (owner // N_COL) * TR + first_row
    cols_at = (owner % N_COL) * TC + first_col
    patch_rows = jnp.arange(16, dtype=jnp.int32)
    patch_cols = jnp.arange(24, dtype=jnp.int32)

    def add_partition(source, canvas):
        begin = (source * RECT_DEV).astype(jnp.int32)
        rows_part = lax.dynamic_slice_in_dim(row_cover, begin, RECT_DEV, 0)
        cols_part = lax.dynamic_slice_in_dim(col_cover, begin, RECT_DEV, 0)
        row_base = lax.dynamic_slice_in_dim(rows_at, begin, RECT_DEV, 0)
        col_base = lax.dynamic_slice_in_dim(cols_at, begin, RECT_DEV, 0)
        patches = rows_part[:, :, None] * cols_part[:, None, :]
        row_index = row_base[:, None, None] + patch_rows[None, :, None] + 0 * patch_cols[None, None, :]
        col_index = col_base[:, None, None] + patch_cols[None, None, :] + 0 * patch_rows[None, :, None]
        return canvas.at[row_index, col_index].add(patches)

    canvas = jnp.zeros((H + 16, W + 24), jnp.float32)
    canvas = lax.fori_loop(0, DEVICES, add_partition, canvas)
    mask = canvas[:H, :W].astype(jnp.bfloat16)

    mask_pad = jnp.pad(mask.astype(jnp.float32), 2 * RAD)
    target_float = target.astype(jnp.float32)
    weighted_target = loss_weight * target_float
    weight_pad = jnp.pad(loss_weight, RAD)
    wtarget_pad = jnp.pad(weighted_target, RAD)
    kernel_float = kernel.astype(jnp.float32)
    flipped = kernel_float[:, ::-1, ::-1][None]
    pair_weight = jnp.repeat(socs_weight, 2)

    def strip(column_block):
        col_start = (column_block * TC).astype(jnp.int32)
        zero_index = jnp.zeros((), jnp.int32)
        mask_part = lax.dynamic_slice(mask_pad, (zero_index, col_start), (H + 4 * RAD, TC + 4 * RAD))
        fields = lax.conv_general_dilated(mask_part[None, None], kernel_float[:, None], (1, 1), "VALID", precision=lax.Precision.HIGHEST)[0]
        weight_part = lax.dynamic_slice(weight_pad, (zero_index, col_start), (H + 2 * RAD, TC + 2 * RAD))
        wtarget_part = lax.dynamic_slice(wtarget_pad, (zero_index, col_start), (H + 2 * RAD, TC + 2 * RAD))
        squared = (fields * fields).reshape(NK, 2, H + 2 * RAD, TC + 2 * RAD)
        intensity = jnp.sum(socs_weight[:, None, None, None] * squared, axis=(0, 1))
        resist = jax.nn.sigmoid(intensity - 3.0)
        slope = 2.0 * (weight_part * resist - wtarget_part) * resist * (1.0 - resist)
        gradient_fields = (2.0 * pair_weight[:, None, None] * fields * slope[None]).astype(jnp.bfloat16)
        gradient_fields = lax.optimization_barrier(gradient_fields).astype(jnp.float32)
        grad_part = lax.conv_general_dilated(gradient_fields[None], flipped, (1, 1), "VALID", precision=lax.Precision.HIGHEST)[0, 0]
        inner = resist[RAD:RAD + H, RAD:RAD + TC]
        weight_inner = lax.dynamic_slice_in_dim(loss_weight, col_start, TC, 1)
        target_inner = lax.dynamic_slice_in_dim(target_float, col_start, TC, 1)
        loss_part = jnp.sum(weight_inner * (inner - target_inner) ** 2)
        return grad_part, loss_part

    grads, loss_parts = lax.map(strip, jnp.arange(N_COL, dtype=jnp.int32))
    mask_grad = jnp.transpose(grads, (1, 0, 2)).reshape(H, W)
    loss = (jnp.sum(loss_parts) / (H * W)).reshape(1)
    return mask_grad, loss
```

```python
import jax
import jax.numpy as jnp
from jax import lax
from jax.experimental import pallas as pl
from jax.experimental.pallas import tpu as pltpu
from jax.sharding import PartitionSpec as P

RAD = 16
CAP = 8
KS = 33
BLK = 32
AROWS = 36
PITCH = 20
NEIGHBOURS = [(dr, dc) for dr in (-1, 0, 1) for dc in (-1, 0, 1) if (dr, dc) != (0, 0)]
F32 = jnp.float32
BF16 = jnp.bfloat16
VMEM_LIMIT = 48 * 1024 * 1024


def dot_nt(a, b):
    return lax.dot_general(a, b, (((1,), (1,)), ((), ())), preferred_element_type=F32)


def iota(shape, dim):
    return lax.broadcasted_iota(jnp.int32, shape, dim)


def outbox_kernel(tile_cols, counts_ref, rects_ref, owner_ref, out_ref, pad_ref):
    slots = owner_ref.shape[1]
    tiles = out_ref.shape[0]
    live = iota((1, slots), 1) < counts_ref[0]
    own = jnp.where(live, owner_ref[...], -1)
    hit = iota((tiles, slots), 0) == own
    hits = jnp.where(hit, 1.0, 0.0).astype(BF16)
    before = jnp.where(iota((slots, slots), 0) < iota((slots, slots), 1), 1.0, 0.0).astype(BF16)
    earlier = jnp.dot(hits, before, preferred_element_type=F32)
    rank = jnp.sum(jnp.where(hit, earlier, 0.0), axis=0, keepdims=True).astype(jnp.int32)
    row = iota((128, slots), 0)
    chosen = rank == ((row >> 1) & 7)
    vertical = (row & 1) == 1

    def placed(first, second):
        value = jnp.where(vertical, second, first)
        value = jnp.where(chosen, value, 0)
        high = (value >> 4).astype(F32).astype(BF16)
        low = (value & 15).astype(F32).astype(BF16)
        return (16.0 * dot_nt(hits, high) + dot_nt(hits, low)).astype(jnp.int32)

    lower = placed(rects_ref[0:1, :], rects_ref[2:3, :])
    upper = placed(rects_ref[1:2, :], rects_ref[3:4, :])
    word = lower + (upper << 16)
    pad_ref[...] = jnp.zeros(pad_ref.shape, jnp.int32)
    pad_ref[24 : 24 + tiles, :] = word
    column = iota((tiles, 128), 0) % tile_cols
    group = iota((tiles, 128), 1) >> 4
    result = jnp.zeros((tiles, 128), jnp.int32)
    for n, (dr, dc) in enumerate(NEIGHBOURS):
        start = 24 + dr * tile_cols + dc
        inside = (column + dc >= 0) & (column + dc < tile_cols) & (group == n)
        result = jnp.where(inside, pad_ref[start : start + tiles, :], result)
    out_ref[:, 0, :] = result
    out_ref[:, 1, :] = word


def make_outbox(rects, owner, counts, tiles, tile_cols):
    slots = owner.shape[0]
    return pl.pallas_call(
        lambda *refs: outbox_kernel(tile_cols, *refs),
        out_shape=jax.ShapeDtypeStruct((tiles, 2, 128), jnp.int32),
        in_specs=[
            pl.BlockSpec(memory_space=pltpu.SMEM),
            pl.BlockSpec(memory_space=pltpu.VMEM),
            pl.BlockSpec(memory_space=pltpu.VMEM),
        ],
        scratch_shapes=[pltpu.VMEM((tiles + 48, 128), jnp.int32)],
        cost_estimate=pl.CostEstimate(flops=10**8, bytes_accessed=10**5, transcendentals=0),
    )(counts, rects, owner.reshape(1, slots))


def toeplitz_pair(taps, edge):
    shape = (BLK, 128)
    rolled = pltpu.roll(jnp.broadcast_to(taps, shape), 0, 1, stride=1, stride_axis=0)
    p = iota(shape, 0)
    co = iota(shape, 1) & (BLK - 1)
    near = jnp.where(co >= p, rolled, 0.0)
    far = pltpu.roll(jnp.where(co < p, rolled, 0.0), 128 - BLK, 1)
    far = far + jnp.where(co == p, jnp.broadcast_to(edge, shape), 0.0)
    return near.astype(BF16), far.astype(BF16)


def tables_kernel(uf_ref, df_ref, ua_ref, da_ref, wf_ref, t_ref):
    def forward_row(a, carry):
        for h in range(2):
            lanes = slice(128 * h, 128 * h + 128)
            near, far = toeplitz_pair(uf_ref[a, :, lanes], df_ref[a, :, lanes])
            wf_ref[a, 0:BLK, lanes] = far
            wf_ref[a, BLK : 2 * BLK, lanes] = near
        return carry

    lax.fori_loop(0, AROWS, forward_row, 0)
    channels = 8

    def adjoint_row(j, carry):
        c, turn = j // 4, j % 4
        rows = pl.ds(pl.multiple_of(c * BLK, BLK), BLK)
        for q in range(ua_ref.shape[2] // 128):
            lanes = slice(128 * q, 128 * q + 128)
            near, far = toeplitz_pair(ua_ref[j, :, lanes], da_ref[j, :, lanes])
            t_ref[0, turn, rows, lanes] = far
            t_ref[1, turn, rows, lanes] = near
        return carry

    lax.fori_loop(0, 4 * channels, adjoint_row, 0)


def make_tables(kernel):
    channels = kernel.shape[0]
    k = kernel.astype(F32)
    by_row = jnp.pad(k.transpose(1, 0, 2), ((0, AROWS - KS), (0, 0), (0, 0)))
    uf = by_row[:, :, KS - 1 : 0 : -1].reshape(AROWS, 1, channels * BLK)
    df = jnp.repeat(by_row[:, :, 0], BLK, axis=1).reshape(AROWS, 1, channels * BLK)
    padded = jnp.pad(k, ((0, 0), (7, 11), (0, 0)))
    turns = jnp.stack([padded[:, t : t + 48] for t in range(4)], axis=1)
    ua = turns[..., : KS - 1].reshape(channels * 4, 1, 48 * BLK)
    da = jnp.repeat(turns[..., KS - 1], BLK, axis=2).reshape(channels * 4, 1, 48 * BLK)
    return pl.pallas_call(
        tables_kernel,
        out_shape=(
            jax.ShapeDtypeStruct((AROWS, 2 * BLK, channels * BLK), BF16),
            jax.ShapeDtypeStruct((2, 4, channels * BLK, 48 * BLK), BF16),
        ),
        compiler_params=pltpu.CompilerParams(vmem_limit_bytes=VMEM_LIMIT),
        cost_estimate=pl.CostEstimate(flops=10**8, bytes_accessed=8 * 10**6, transcendentals=0),
    )(uf, df, ua, da)


def weights_kernel(center_ref, top_ref, bottom_ref, left_ref, right_ref, sw_ref, lw_ref, x_ref):
    rows, cols = center_ref.shape
    ext = rows + 2 * RAD
    x_ref[0:RAD, 0:cols] = top_ref[...]
    x_ref[RAD : RAD + rows, 0:cols] = center_ref[...]
    x_ref[RAD + rows : ext, 0:cols] = bottom_ref[...]
    x_ref[:, cols : cols + RAD] = right_ref[...]
    sw_ref[...] = jnp.zeros(sw_ref.shape, F32)
    lw_ref[...] = jnp.zeros(lw_ref.shape, F32)
    blocks = cols // BLK + 1
    r = iota((ext, 128), 0)
    own_rows = (r >= RAD) & (r < RAD + rows)
    co = iota((ext, 128), 1) & (BLK - 1)
    for b in range(blocks):
        if b == 0:
            piece = jnp.concatenate([left_ref[...], x_ref[:, 0:RAD]], axis=1)
        else:
            piece = x_ref[:, BLK * b - RAD : BLK * b + RAD]
        piece = jnp.concatenate([piece] * 4, axis=1)
        own = own_rows
        if b == 0:
            own = own & (co >= RAD)
        if b == blocks - 1:
            own = own & (co < RAD)
        sw_ref[pl.ds(b, ext, stride=PITCH), :] = piece
        lw_ref[pl.ds(b, ext, stride=PITCH), :] = jnp.where(own, 0.25 * jnp.abs(piece), 0.0)


def make_weights(target, loss_weight):
    rows, cols = target.shape
    signed = jnp.where(target > 0, loss_weight, -loss_weight)

    def beside(x, axis, dim):
        count, length = lax.axis_size(axis), x.shape[dim]
        up = [(i, i + 1) for i in range(count - 1)]
        down = [(j, i) for i, j in up]
        before = lax.ppermute(lax.slice_in_dim(x, length - RAD, length, axis=dim), axis, up)
        after = lax.ppermute(lax.slice_in_dim(x, 0, RAD, axis=dim), axis, down)
        return before, after

    top, bottom = beside(signed, "row", 0)
    ends = jnp.concatenate([signed[:, :RAD], signed[:, cols - RAD :]], axis=1)
    corner = [jnp.concatenate([x[:, :RAD], x[:, cols - RAD :]], axis=1) for x in (top, bottom)]
    ends = jnp.concatenate([corner[0], ends, corner[1]], axis=0)
    left, right = beside(ends, "col", 1)
    ext = rows + 2 * RAD
    shape = jax.ShapeDtypeStruct((ext * PITCH, 128), F32)
    return pl.pallas_call(
        weights_kernel,
        out_shape=(shape, shape),
        scratch_shapes=[pltpu.VMEM((ext, cols + 128), F32)],
        compiler_params=pltpu.CompilerParams(vmem_limit_bytes=VMEM_LIMIT),
        cost_estimate=pl.CostEstimate(flops=10**7, bytes_accessed=4 * 10**6, transcendentals=0),
    )(signed, top, bottom, left, right)


def imaging_kernel(rows, cols, inbox_ref, wf_ref, sw_ref, lw_ref, wv_ref, g_ref, loss_ref, mask_ref, s_ref, a_ref, gs_ref):
    halo = 2 * RAD
    ext = rows + 2 * RAD
    tall = rows + 2 * halo
    words = [inbox_ref[:, 0, :].T, inbox_ref[:, 1, :].T]
    lower = [(x & 0xFFFF).astype(F32) * 0.25 for x in words]
    upper = [(x >> 16).astype(F32) * 0.25 for x in words]

    def covers(group, base, first, count):
        cell = iota((count, 128), 0).astype(F32) + float(first)
        parts = []
        for rank in range(CAP):
            at = base + 2 * rank
            low, high = lower[group][at : at + 1, :], upper[group][at : at + 1, :]
            parts.append((jnp.clip(high - cell, 0.0, 1.0) - jnp.clip(low - cell, 0.0, 1.0)).astype(BF16))
        return jnp.concatenate(parts, axis=1)

    row_span = {-1: (rows - halo, halo, 0), 0: (0, rows, halo), 1: (0, halo, halo + rows)}
    col_span = {-1: (cols - halo, halo, cols + halo), 0: (0, cols, 0), 1: (0, halo, cols)}
    for n, (dr, dc) in enumerate(NEIGHBOURS + [(0, 0)]):
        group, base = (1, 0) if n == 8 else (0, 16 * n)
        r_first, r_count, r_at = row_span[dr]
        c_first, c_count, c_at = col_span[dc]
        row_cover = covers(group, base + 1, r_first, r_count)
        col_cover = covers(group, base, c_first, c_count)
        part = dot_nt(row_cover, col_cover).astype(BF16).astype(F32)
        mask_ref[r_at : r_at + r_count, c_at : c_at + c_count] = part

    s_ref[...] = jnp.zeros(s_ref.shape, F32)
    blocks = cols // BLK + 1
    for b in range(blocks):
        if b == 0:
            window = jnp.concatenate([mask_ref[:, cols + halo : cols + 2 * halo], mask_ref[:, 0:BLK]], axis=1)
        else:
            window = mask_ref[:, BLK * (b - 1) : BLK * (b + 1)]
        s_ref[pl.ds(b, tall, stride=PITCH), :] = jnp.concatenate([window, window], axis=1)
    step = 16 * PITCH
    first_half = iota((step, 128), 1) < 64
    for m in range(0, tall * PITCH, step):
        for h in range(2):
            even = s_ref[m + 2 * h * PITCH : m + 2 * h * PITCH + step, :]
            odd = s_ref[m + (2 * h + 1) * PITCH : m + (2 * h + 1) * PITCH + step, :]
            a_ref[m : m + step, 128 * h : 128 * h + 128] = jnp.where(first_half, even, odd).astype(BF16)

    wv = wv_ref[...]
    total = jnp.zeros((1, 128), F32)
    chunk_rows = ext // 4
    chunk = chunk_rows * PITCH
    for k in range(4):
        m = k * chunk
        fields = jnp.zeros((chunk, 256), F32)
        for g in range(AROWS // 4):
            fields = fields + jnp.dot(
                a_ref[m + 4 * PITCH * g : m + 4 * PITCH * g + chunk, :],
                wf_ref[256 * g : 256 * g + 256, :],
                preferred_element_type=F32,
            )
        square = fields * fields * wv
        intensity = square[:, :128] + square[:, 128:]
        intensity = intensity + pltpu.roll(intensity, 64, 1)
        intensity = intensity + pltpu.roll(intensity, 32, 1)
        resist = 1.0 / (1.0 + jnp.exp(3.0 - intensity))
        signed = sw_ref[m : m + chunk, :]
        slope = 2.0 * (jnp.abs(signed) * resist - jnp.maximum(signed, 0.0)) * resist * (1.0 - resist)
        miss = resist - jnp.where(signed > 0.0, 1.0, 0.0)
        total = total + jnp.sum(lw_ref[m : m + chunk, :] * miss * miss, axis=0, keepdims=True)
        gs_ref[m : m + chunk, 0:128] = (2.0 * wv[:, :128]) * fields[:, :128] * slope
        gs_ref[m : m + chunk, 128:256] = (2.0 * wv[:, 128:]) * fields[:, 128:] * slope
        for r in range(k * chunk_rows, (k + 1) * chunk_rows):
            for s in range(2):
                at = r * PITCH + s
                g_ref[s, r % 8, r // 8] = gs_ref[at : at + 16, :].astype(BF16)
    loss_ref[...] = jnp.broadcast_to(jnp.sum(total, axis=1, keepdims=True), loss_ref.shape)


def imaging(inbox, wf, sw, lw, socs_weight, rows, cols, channels):
    ext = rows + 2 * RAD
    tall = rows + 4 * RAD
    wv = jnp.repeat(socs_weight, 2 * BLK).reshape(1, channels * BLK)
    return pl.pallas_call(
        lambda *refs: imaging_kernel(rows, cols, *refs),
        out_shape=(
            jax.ShapeDtypeStruct((2, 8, ext // 8, 16, channels * BLK), BF16),
            jax.ShapeDtypeStruct((1, 128), F32),
        ),
        scratch_shapes=[
            pltpu.VMEM((tall, cols + 128), F32),
            pltpu.VMEM(((tall + 4) * PITCH, 128), F32),
            pltpu.VMEM((tall * PITCH, 256), BF16),
            pltpu.VMEM((ext * PITCH, 256), F32),
        ],
        compiler_params=pltpu.CompilerParams(vmem_limit_bytes=VMEM_LIMIT),
        cost_estimate=pl.CostEstimate(flops=4 * 10**9, bytes_accessed=8 * 10**6, transcendentals=10**6),
    )(inbox, wf.reshape(AROWS * 2 * BLK, channels * BLK), sw, lw, wv)


def adjoint_kernel(g_ref, t_ref, out_ref):
    total = jnp.zeros(out_ref.shape, F32)
    for i in range(40):
        q, turn = divmod(39 - i, 4)
        for s in range(2):
            left = g_ref[s, i % 8, i // 8 : i // 8 + 16].reshape(256, 256)
            total = total + jnp.dot(left, t_ref[s, turn, :, 128 * q : 128 * q + 256], preferred_element_type=F32)
    out_ref[...] = total


def adjoint(g, tables, rows, cols):
    out = pl.pallas_call(
        adjoint_kernel,
        out_shape=jax.ShapeDtypeStruct((256, 256), F32),
        compiler_params=pltpu.CompilerParams(vmem_limit_bytes=VMEM_LIMIT),
        cost_estimate=pl.CostEstimate(flops=4 * 10**9, bytes_accessed=10**7, transcendentals=0),
    )(g, tables)
    return out.reshape(rows // 8, cols // BLK, 8, BLK).transpose(0, 2, 1, 3).reshape(rows, cols)


def shards(rects, owner, counts, target, loss_weight, kernel, socs_weight):
    row_devices = lax.axis_size("row")
    col_devices = lax.axis_size("col")
    devices = row_devices * col_devices
    rows, cols = target.shape
    outbox = make_outbox(rects, owner, counts, devices, col_devices)
    inbox = lax.all_to_all(outbox, ("row", "col"), split_axis=0, concat_axis=0, tiled=True)
    wf, tables = make_tables(kernel)
    sw, lw = make_weights(target, loss_weight)
    g, local = imaging(inbox, wf, sw, lw, socs_weight, rows, cols, kernel.shape[0])
    losses = lax.all_to_all(local.reshape(devices), ("row", "col"), split_axis=0, concat_axis=0, tiled=True)
    mask_grad = adjoint(g, tables, rows, cols)
    window_area = rows * row_devices * cols * col_devices
    return (mask_grad, (jnp.sum(losses) / window_area).reshape(1))


def solution(mesh):
    placed = (
        P(None, ("row", "col")),
        P(("row", "col")),
        P(("row", "col")),
        P("row", "col"),
        P("row", "col"),
        P(),
        P(),
    )
    return jax.shard_map(
        shards, mesh=mesh, in_specs=placed, out_specs=(P("row", "col"), P()), check_vma=False
    )
```

```python
import jax
import jax.numpy as jnp
from jax import lax
from jax.experimental import pallas as pl
from jax.experimental.pallas import tpu as pltpu
from jax.sharding import PartitionSpec as P

RAD = 16
CAP = 8
KS = 33
BLK = 32
AROWS = 36
LEAD = 7
TABLE = 47
PITCH = 20
NEIGHBOURS = [(dr, dc) for dr in (-1, 0, 1) for dc in (-1, 0, 1) if (dr, dc) != (0, 0)]
F32 = jnp.float32
BF16 = jnp.bfloat16
VMEM_LIMIT = 32 * 1024 * 1024


def dot_nt(a, b):
    return lax.dot_general(a, b, (((1,), (1,)), ((), ())), preferred_element_type=F32)


def iota(shape, dim):
    return lax.broadcasted_iota(jnp.int32, shape, dim)


def outbox_kernel(tile_cols, counts_ref, rects_ref, owner_ref, out_ref, pad_ref):
    slots = owner_ref.shape[1]
    tiles = out_ref.shape[0]
    live = iota((1, slots), 1) < counts_ref[0]
    own = jnp.where(live, owner_ref[...], -1)
    hit = iota((tiles, slots), 0) == own
    hits = jnp.where(hit, 1.0, 0.0).astype(BF16)
    before = jnp.where(iota((slots, slots), 0) < iota((slots, slots), 1), 1.0, 0.0).astype(BF16)
    earlier = jnp.dot(hits, before, preferred_element_type=F32)
    rank = jnp.sum(jnp.where(hit, earlier, 0.0), axis=0, keepdims=True).astype(jnp.int32)
    row = iota((128, slots), 0)
    chosen = rank == (row & 7)
    vertical = (row & 8) == 8

    def placed(first, second):
        value = jnp.where(vertical, second, first)
        value = jnp.where(chosen, value, 0)
        high = (value >> 4).astype(F32).astype(BF16)
        low = (value & 15).astype(F32).astype(BF16)
        return (16.0 * dot_nt(hits, high) + dot_nt(hits, low)).astype(jnp.int32)

    lower = placed(rects_ref[0:1, :], rects_ref[2:3, :])
    upper = placed(rects_ref[1:2, :], rects_ref[3:4, :])
    word = lower + (upper << 16)
    pad_ref[...] = jnp.zeros(pad_ref.shape, jnp.int32)
    pad_ref[24 : 24 + tiles, :] = word
    column = iota((tiles, 128), 0) % tile_cols
    group = iota((tiles, 128), 1) >> 4
    result = jnp.zeros((tiles, 128), jnp.int32)
    for n, (dr, dc) in enumerate(NEIGHBOURS):
        start = 24 + dr * tile_cols + dc
        inside = (column + dc >= 0) & (column + dc < tile_cols) & (group == n)
        result = jnp.where(inside, pad_ref[start : start + tiles, :], result)
    out_ref[:, 0, :] = result
    out_ref[:, 1, :] = word


def make_outbox(rects, owner, counts, tiles, tile_cols):
    slots = owner.shape[0]
    return pl.pallas_call(
        lambda *refs: outbox_kernel(tile_cols, *refs),
        out_shape=jax.ShapeDtypeStruct((tiles, 2, 128), jnp.int32),
        in_specs=[
            pl.BlockSpec(memory_space=pltpu.SMEM),
            pl.BlockSpec(memory_space=pltpu.VMEM),
            pl.BlockSpec(memory_space=pltpu.VMEM),
        ],
        scratch_shapes=[pltpu.VMEM((tiles + 48, 128), jnp.int32)],
        cost_estimate=pl.CostEstimate(flops=10**8, bytes_accessed=10**5, transcendentals=0),
    )(counts, rects, owner.reshape(1, slots))


def tables_kernel(taps_ref, edge_ref, table_ref):
    zero = jnp.zeros((2 * BLK, table_ref.shape[2]), BF16)
    for a in range(TABLE):
        if a < LEAD or a >= LEAD + KS:
            table_ref[a] = zero
    shape = (BLK, 128)
    p = iota(shape, 0)
    co = iota(shape, 1) & (BLK - 1)
    for a in range(KS):
        for h in range(table_ref.shape[2] // 128):
            lanes = slice(128 * h, 128 * h + 128)
            taps = jnp.broadcast_to(taps_ref[a : a + 1, lanes], shape)
            rolled = pltpu.roll(taps, 0, 1, stride=1, stride_axis=0)
            far = pltpu.roll(jnp.where(co < p, rolled, 0.0), 128 - BLK, 1)
            far = far + jnp.where(co == p, jnp.broadcast_to(edge_ref[a : a + 1, lanes], shape), 0.0)
            table_ref[LEAD + a, 0:BLK, lanes] = far.astype(BF16)
            table_ref[LEAD + a, BLK : 2 * BLK, lanes] = jnp.where(co >= p, rolled, 0.0).astype(BF16)


def make_tables(kernel):
    channels = kernel.shape[0]
    by_row = kernel.astype(F32).transpose(1, 0, 2)
    taps = by_row[:, :, KS - 1 : 0 : -1].reshape(KS, channels * BLK)
    edge = jnp.repeat(by_row[:, :, 0], BLK, axis=1)
    return pl.pallas_call(
        tables_kernel,
        out_shape=pltpu.VMEM((TABLE, 2 * BLK, channels * BLK), BF16),
        compiler_params=pltpu.CompilerParams(vmem_limit_bytes=VMEM_LIMIT // 2),
        cost_estimate=pl.CostEstimate(flops=10**8, bytes_accessed=10**6, transcendentals=0),
    )(taps, edge)


def weight_strips(target, loss_weight):
    rows, cols = target.shape

    def signed(*at):
        return jnp.where(target[at] > 0, loss_weight[at], -loss_weight[at])

    def beside(first, last, axis):
        count = lax.axis_size(axis)
        up = [(i, (i + 1) % count) for i in range(count)]
        down = [(j, i) for i, j in up]
        return lax.ppermute(last, axis, up), lax.ppermute(first, axis, down)

    row_top, row_bottom = slice(0, RAD), slice(rows - RAD, rows)
    col_left, col_right = slice(0, RAD), slice(cols - RAD, cols)
    top, bottom = beside(signed(row_top, slice(None)), signed(row_bottom, slice(None)), "row")
    left, right = beside(
        jnp.concatenate([top[:, col_left], signed(slice(None), col_left), bottom[:, col_left]], axis=0),
        jnp.concatenate([top[:, col_right], signed(slice(None), col_right), bottom[:, col_right]], axis=0),
        "col",
    )
    r, c = lax.axis_index("row"), lax.axis_index("col")
    inside = jnp.stack([r > 0, r < lax.axis_size("row") - 1, c > 0, c < lax.axis_size("col") - 1])
    return top, bottom, left, right, inside.astype(jnp.int32)


def spread(x_ref, left, right, out_ref, rows, cols):
    for b in range(cols // BLK + 1):
        if b == 0:
            piece = jnp.concatenate([left, x_ref[:, 0:RAD]], axis=1)
        elif b == cols // BLK:
            piece = jnp.concatenate([x_ref[:, cols - RAD : cols], right], axis=1)
        else:
            piece = x_ref[:, BLK * b - RAD : BLK * b + RAD]
        out_ref[pl.ds(b, rows, stride=PITCH), :] = jnp.concatenate([piece] * 4, axis=1)
    for b in range(cols // BLK + 1, PITCH):
        out_ref[pl.ds(b, rows, stride=PITCH), :] = jnp.zeros((rows, 128), F32)


def correlate(a_ref, starts, count, table_ref):
    fields = None
    for g in range(AROWS // 4):
        parts = [a_ref[m + 4 * PITCH * g : m + 4 * PITCH * g + count, :] for m in starts]
        left = parts[0] if len(parts) == 1 else jnp.concatenate(parts, axis=0)
        right = table_ref[LEAD + 4 * g : LEAD + 4 * g + 4].reshape(8 * BLK, 256)
        term = jnp.dot(left, right, preferred_element_type=F32)
        fields = term if fields is None else fields + term
    return fields


def resist_and_gradient(fields, signed, wv, gs_ref, at):
    square = fields * fields * wv
    intensity = square[:, :128] + square[:, 128:]
    intensity = intensity + pltpu.roll(intensity, 64, 1)
    intensity = intensity + pltpu.roll(intensity, 32, 1)
    resist = 1.0 / (1.0 + jnp.exp(3.0 - intensity))
    slope = 2.0 * (jnp.abs(signed) * resist - jnp.maximum(signed, 0.0)) * resist * (1.0 - resist)
    for h in range(2):
        lanes = slice(128 * h, 128 * h + 128)
        gs_ref[at : at + fields.shape[0], lanes] = (2.0 * wv[:, lanes]) * fields[:, lanes] * slope
    return resist


def imaging_kernel(
    inbox_ref, table_ref, target_ref, weight_ref, left_ref, right_ref, wv_ref, inside_ref,
    loss_ref, a_ref, gs_ref, mask_ref, s_ref, x_ref, sw_ref,
):
    rows, cols = target_ref.shape
    halo = 2 * RAD
    tall = rows + 2 * halo
    words = [inbox_ref[:, 0, :].T, inbox_ref[:, 1, :].T]
    lower = [(x & 0xFFFF).astype(F32) * 0.25 for x in words]
    upper = [(x >> 16).astype(F32) * 0.25 for x in words]
    cell = iota((BLK, 128), 0).astype(F32).astype(BF16)
    cell_end = (iota((BLK, 128), 0) + 1).astype(F32).astype(BF16)

    def covers(group, at, first, count):
        low8, high8 = lower[group][at : at + CAP, :], upper[group][at : at + CAP, :]
        stacked = []
        for base in range(first, first + count, BLK):
            low = jnp.clip(low8 - float(base), 0.0, float(BLK))
            high = jnp.clip(high8 - float(base), 0.0, float(BLK))
            parts = []
            for rank in range(CAP):
                lo = jnp.broadcast_to(low[rank : rank + 1, :], (BLK, 128)).astype(BF16)
                hi = jnp.broadcast_to(high[rank : rank + 1, :], (BLK, 128)).astype(BF16)
                parts.append(jnp.maximum(jnp.minimum(hi, cell_end) - jnp.maximum(lo, cell), 0.0))
            stacked.append(jnp.concatenate(parts, axis=1))
        return stacked[0] if len(stacked) == 1 else jnp.concatenate(stacked, axis=0)

    row_span = {-1: (rows - halo, halo, 0), 0: (0, rows, halo), 1: (0, halo, halo + rows)}
    col_span = {-1: (cols - halo, halo, cols + halo), 0: (0, cols, 0), 1: (0, halo, cols)}
    for n, (dr, dc) in enumerate(NEIGHBOURS + [(0, 0)]):
        group, at = (1, 0) if n == 8 else (0, 16 * n)
        r_first, r_count, r_at = row_span[dr]
        c_first, c_count, c_at = col_span[dc]
        row_cover = covers(group, at + 8, r_first, r_count)
        col_cover = covers(group, at, c_first, c_count)
        part = dot_nt(row_cover, col_cover).astype(BF16).astype(F32)
        mask_ref[r_at : r_at + r_count, c_at : c_at + c_count] = part

    s_ref[...] = jnp.zeros(s_ref.shape, F32)
    for b in range(cols // BLK + 1):
        if b == 0:
            window = jnp.concatenate([mask_ref[:, cols + halo : cols + 2 * halo], mask_ref[:, 0:BLK]], axis=1)
        else:
            window = mask_ref[:, BLK * (b - 1) : BLK * (b + 1)]
        s_ref[pl.ds(b, tall, stride=PITCH), :] = jnp.concatenate([window, window], axis=1)
    step = 16 * PITCH
    first_half = iota((step, 128), 1) < 64
    for m in range(0, tall * PITCH, step):
        for h in range(2):
            even = s_ref[m + 2 * h * PITCH : m + 2 * h * PITCH + step, :]
            odd = s_ref[m + (2 * h + 1) * PITCH : m + (2 * h + 1) * PITCH + step, :]
            a_ref[m : m + step, 128 * h : 128 * h + 128] = jnp.where(first_half, even, odd).astype(BF16)

    x_ref[...] = jnp.where(target_ref[...] > 0, weight_ref[...], -weight_ref[...])
    left = jnp.where(inside_ref[2] > 0, left_ref[RAD : RAD + rows, :], 0.0)
    right = jnp.where(inside_ref[3] > 0, right_ref[RAD : RAD + rows, :], 0.0)
    spread(x_ref, left, right, sw_ref, rows, cols)

    wv = wv_ref[...]
    chunk = rows // 4 * PITCH
    block = iota((chunk, 128), 0) % PITCH
    co = iota((chunk, 128), 1) & (BLK - 1)
    own = ((block > 0) | (co >= RAD)) & ((block < cols // BLK) | (co < RAD)) & (block <= cols // BLK)
    total = jnp.zeros((1, 128), F32)
    for k in range(4):
        m = k * chunk
        fields = correlate(a_ref, [RAD * PITCH + m], chunk, table_ref)
        signed = sw_ref[m : m + chunk, :]
        resist = resist_and_gradient(fields, signed, wv, gs_ref, m)
        miss = resist - jnp.where(signed > 0.0, 1.0, 0.0)
        part = jnp.where(own, jnp.abs(signed), 0.0) * miss * miss
        total = total + jnp.sum(part, axis=0, keepdims=True)
    total = 0.25 * jnp.sum(total, axis=1, keepdims=True)
    loss_ref[...] = jnp.broadcast_to(total, loss_ref.shape)


SMALL = pl.BlockSpec(memory_space=pltpu.SMEM)
WHOLE = pl.BlockSpec(memory_space=pltpu.VMEM)


def imaging(inbox, table, target, weight, left, right, wv, inside):
    rows, cols = target.shape
    tall = rows + 4 * RAD
    return pl.pallas_call(
        imaging_kernel,
        out_shape=(
            jax.ShapeDtypeStruct((1, 128), F32),
            pltpu.VMEM((tall * PITCH, 256), BF16),
            pltpu.VMEM((rows * PITCH, 256), F32),
        ),
        in_specs=[WHOLE] * 7 + [SMALL],
        scratch_shapes=[
            pltpu.VMEM((tall, cols + 128), F32),
            pltpu.VMEM(((tall + 4) * PITCH, 128), F32),
            pltpu.VMEM((rows, cols), F32),
            pltpu.VMEM((rows * PITCH, 128), F32),
        ],
        compiler_params=pltpu.CompilerParams(vmem_limit_bytes=VMEM_LIMIT),
        cost_estimate=pl.CostEstimate(flops=4 * 10**9, bytes_accessed=8 * 10**6, transcendentals=10**6),
    )(inbox, table, target, weight, left, right, wv, inside)


def adjoint_kernel(
    a_ref, table_ref, gs_ref, top_ref, bottom_ref, left_ref, right_ref, wv_ref, inside_ref,
    out_ref, x_ref, sw_ref, gh_ref, g_ref, acc_ref, tile_ref,
):
    rows, cols = out_ref.shape
    ext = rows + 2 * RAD
    x_ref[0:RAD, :] = jnp.where(inside_ref[0] > 0, top_ref[...], 0.0)
    x_ref[RAD : 2 * RAD, :] = jnp.where(inside_ref[1] > 0, bottom_ref[...], 0.0)

    def corners(ref, flag):
        first = jnp.where((inside_ref[flag] > 0) & (inside_ref[0] > 0), ref[0:RAD, :], 0.0)
        last = jnp.where((inside_ref[flag] > 0) & (inside_ref[1] > 0), ref[ext - RAD : ext, :], 0.0)
        return jnp.concatenate([first, last], axis=0)

    spread(x_ref, corners(left_ref, 2), corners(right_ref, 3), sw_ref, 2 * RAD, cols)
    fields = correlate(a_ref, [0, (rows + RAD) * PITCH], RAD * PITCH, table_ref)
    resist_and_gradient(fields, sw_ref[...], wv_ref[...], gh_ref, 0)

    for r in range(ext):
        for s in range(2):
            if r < RAD:
                source, at = gh_ref, r * PITCH + s
            elif r >= RAD + rows:
                source, at = gh_ref, (r - rows) * PITCH + s
            else:
                source, at = gs_ref, (r - RAD) * PITCH + s
            g_ref[s, r % 8, r // 8] = source[at : at + 16, :].astype(BF16)

    total = jnp.zeros((256, 256), F32)
    for i in range(40):
        for s in range(2):
            fields = g_ref[s, i % 8, i // 8 : i // 8 + 16].reshape(256, 256)
            taps = table_ref[39 - i : 47 - i, BLK * (1 - s) : BLK * (2 - s), :].reshape(256, 256)
            total = total + dot_nt(fields, taps)
    for h in range(2):
        acc_ref[h] = total[:, 128 * h : 128 * h + 128]
    for q in range(cols // 128):
        for h in range(2):
            per_block = [acc_ref[h, pl.ds(4 * q + j, 16, stride=16), :] for j in range(4)]
            for j in range(4):
                pieces = [x[:, BLK * j : BLK * j + BLK] for x in per_block]
                tile_ref[q, pl.ds(4 * h + j, 16, stride=8), :] = jnp.concatenate(pieces, axis=1)
        out_ref[:, 128 * q : 128 * q + 128] = tile_ref[q]


def adjoint(a, table, gs, top, bottom, left, right, wv, inside, rows, cols):
    ext = rows + 2 * RAD
    return pl.pallas_call(
        adjoint_kernel,
        out_shape=jax.ShapeDtypeStruct((rows, cols), F32),
        in_specs=[WHOLE] * 8 + [SMALL],
        scratch_shapes=[
            pltpu.VMEM((2 * RAD, cols), F32),
            pltpu.VMEM((2 * RAD * PITCH, 128), F32),
            pltpu.VMEM((2 * RAD * PITCH, 256), F32),
            pltpu.VMEM((2, 8, ext // 8, 16, 256), BF16),
            pltpu.VMEM((2, 256, 128), F32),
            pltpu.VMEM((cols // 128, rows, 128), F32),
        ],
        compiler_params=pltpu.CompilerParams(vmem_limit_bytes=VMEM_LIMIT),
        cost_estimate=pl.CostEstimate(flops=4 * 10**9, bytes_accessed=10**7, transcendentals=0),
    )(a, table, gs, top, bottom, left, right, wv, inside)


def shards(rects, owner, counts, target, loss_weight, kernel, socs_weight):
    row_devices = lax.axis_size("row")
    col_devices = lax.axis_size("col")
    devices = row_devices * col_devices
    rows, cols = target.shape
    outbox = make_outbox(rects, owner, counts, devices, col_devices)
    inbox = lax.all_to_all(outbox, ("row", "col"), split_axis=0, concat_axis=0, tiled=True)
    table = make_tables(kernel)
    top, bottom, left, right, inside = weight_strips(target, loss_weight)
    wv = jnp.repeat(socs_weight, 2 * BLK).reshape(1, 256)
    local, a, gs = imaging(inbox, table, target, loss_weight, left, right, wv, inside)
    losses = lax.all_to_all(local.reshape(devices), ("row", "col"), split_axis=0, concat_axis=0, tiled=True)
    mask_grad = adjoint(a, table, gs, top, bottom, left, right, wv, inside, rows, cols)
    window_area = rows * row_devices * cols * col_devices
    return (mask_grad, (jnp.sum(losses) / window_area).reshape(1))


def solution(mesh):
    placed = (
        P(None, ("row", "col")),
        P(("row", "col")),
        P(("row", "col")),
        P("row", "col"),
        P("row", "col"),
        P(),
        P(),
    )
    return jax.shard_map(
        shards, mesh=mesh, in_specs=placed, out_specs=(P("row", "col"), P()), check_vma=False
    )
```

```python
import jax
import jax.numpy as jnp
from jax import lax
from jax.experimental import pallas as pl
from jax.experimental.pallas import tpu as pltpu
from jax.sharding import PartitionSpec as P

RAD = 16
CAP = 8
KS = 33
BLK = 32
AROWS = 36
LEAD = 7
TABLE = 47
WIDE = 2 * BLK + 1
PITCH = 20
NEIGHBOURS = [(dr, dc) for dr in (-1, 0, 1) for dc in (-1, 0, 1) if (dr, dc) != (0, 0)]
F32 = jnp.float32
BF16 = jnp.bfloat16
VMEM_LIMIT = 32 * 1024 * 1024


def dot_nt(a, b):
    return lax.dot_general(a, b, (((1,), (1,)), ((), ())), preferred_element_type=F32)


def iota(shape, dim):
    return lax.broadcasted_iota(jnp.int32, shape, dim)


def outbox_kernel(
    tile_cols, counts_ref, rects_ref, owner_ref, target_ref, weight_ref,
    out_ref, signed_ref, top_ref, bottom_ref, left_ref, right_ref,
    pad_ref, target_buf, weight_buf, sems,
):
    rows, cols = signed_ref.shape
    load_target = pltpu.make_async_copy(target_ref, target_buf, sems.at[0])
    load_weight = pltpu.make_async_copy(weight_ref, weight_buf, sems.at[1])
    load_target.start()
    load_weight.start()
    slots = owner_ref.shape[1]
    tiles = out_ref.shape[0]
    live = iota((1, slots), 1) < counts_ref[0]
    own = jnp.where(live, owner_ref[...], -1)
    hit = iota((tiles, slots), 0) == own
    hits = jnp.where(hit, 1.0, 0.0).astype(BF16)
    before = jnp.where(iota((slots, slots), 0) < iota((slots, slots), 1), 1.0, 0.0).astype(BF16)
    earlier = jnp.dot(hits, before, preferred_element_type=F32)
    rank = jnp.sum(jnp.where(hit, earlier, 0.0), axis=0, keepdims=True).astype(jnp.int32)
    row = iota((16, slots), 0)
    chosen = rank == (row & 7)
    vertical = (row & 8) == 8

    def placed(first, second):
        value = jnp.where(vertical, second, first)
        value = jnp.where(chosen, value, 0)
        high = (value >> 4).astype(F32).astype(BF16)
        low = (value & 15).astype(F32).astype(BF16)
        return (16.0 * dot_nt(hits, high) + dot_nt(hits, low)).astype(jnp.int32)

    lower = placed(rects_ref[0:1, :], rects_ref[2:3, :])
    upper = placed(rects_ref[1:2, :], rects_ref[3:4, :])
    word = lower + (upper << 16)
    word = jnp.concatenate([word] * 8, axis=1)
    pad_ref[...] = jnp.zeros(pad_ref.shape, jnp.int32)
    pad_ref[24 : 24 + tiles, :] = word
    column = iota((tiles, 128), 0) % tile_cols
    group = iota((tiles, 128), 1) >> 4
    result = jnp.zeros((tiles, 128), jnp.int32)
    for n, (dr, dc) in enumerate(NEIGHBOURS):
        start = 24 + dr * tile_cols + dc
        inside = (column + dc >= 0) & (column + dc < tile_cols) & (group == n)
        result = jnp.where(inside, pad_ref[start : start + tiles, :], result)
    out_ref[:, 0, :] = result
    out_ref[:, 1, :] = word
    load_target.wait()
    load_weight.wait()
    signed_ref[...] = jnp.where(target_buf[...] > 0, weight_buf[...], -weight_buf[...])
    top_ref[...] = signed_ref[0:RAD, :]
    bottom_ref[...] = signed_ref[rows - RAD : rows, :]
    left_ref[...] = signed_ref[:, 0:RAD]
    right_ref[...] = signed_ref[:, cols - RAD : cols]


SMALL = pl.BlockSpec(memory_space=pltpu.SMEM)
WHOLE = pl.BlockSpec(memory_space=pltpu.VMEM)
ANYWHERE = pl.BlockSpec(memory_space=pl.ANY)


def make_outbox(rects, owner, counts, target, weight, tiles, tile_cols):
    slots = owner.shape[0]
    rows, cols = target.shape
    return pl.pallas_call(
        lambda *refs: outbox_kernel(tile_cols, *refs),
        out_shape=(
            pltpu.VMEM((tiles, 2, 128), jnp.int32),
            pltpu.VMEM((rows, cols), F32),
            pltpu.VMEM((RAD, cols), F32),
            pltpu.VMEM((RAD, cols), F32),
            pltpu.VMEM((rows, RAD), F32),
            pltpu.VMEM((rows, RAD), F32),
        ),
        in_specs=[SMALL, WHOLE, WHOLE, ANYWHERE, ANYWHERE],
        scratch_shapes=[
            pltpu.VMEM((tiles + 48, 128), jnp.int32),
            pltpu.VMEM((rows, cols), jnp.int32),
            pltpu.VMEM((rows, cols), F32),
            pltpu.SemaphoreType.DMA((2,)),
        ],
        cost_estimate=pl.CostEstimate(flops=10**8, bytes_accessed=10**6, transcendentals=0),
    )(counts, rects, owner.reshape(1, slots), target, weight)


def tables_kernel(kernel_ref, table_ref, wide_ref):
    channels = kernel_ref.shape[0]
    lanes = channels * BLK
    tap, lane = iota((KS, lanes), 0), iota((KS, lanes), 1)
    taps = jnp.zeros((KS, lanes), F32)
    edge = jnp.zeros((KS, lanes), F32)
    for c in range(channels):
        mine = lane // BLK == c
        reverse = jnp.where(mine & (tap == KS - 1 - lane % BLK), 1.0, 0.0).astype(BF16)
        first = jnp.where(mine & (tap == 0), 1.0, 0.0).astype(BF16)
        taps = taps + jnp.dot(kernel_ref[c], reverse, preferred_element_type=F32)
        edge = edge + jnp.dot(kernel_ref[c], first, preferred_element_type=F32)
    co = iota((KS, 128), 1) % BLK
    for p in range(BLK):
        for h in range(lanes // 128):
            mine = taps[:, 128 * h : 128 * h + 128]
            ends = edge[:, 128 * h : 128 * h + 128]
            near = pltpu.roll(mine, p, 1) if p else mine
            far = pltpu.roll(mine, p + 128 - BLK, 1)
            far = jnp.where(co < p, far, jnp.where(co == p, ends, 0.0))
            wide_ref[h, pl.ds(p, KS, stride=WIDE), :] = far
            wide_ref[h, pl.ds(BLK + p, KS, stride=WIDE), :] = jnp.where(co >= p, near, 0.0)
    zero = jnp.zeros((2 * BLK, lanes), BF16)
    for a in range(TABLE):
        if a < LEAD or a >= LEAD + KS:
            table_ref[a] = zero
            continue
        at = (a - LEAD) * WIDE
        for h in range(lanes // 128):
            table_ref[a, :, 128 * h : 128 * h + 128] = wide_ref[h, at : at + 2 * BLK, :].astype(BF16)


def make_tables(kernel):
    lanes = kernel.shape[0] * BLK
    return pl.pallas_call(
        tables_kernel,
        out_shape=pltpu.VMEM((TABLE, 2 * BLK, lanes), BF16),
        in_specs=[WHOLE],
        scratch_shapes=[pltpu.VMEM((lanes // 128, KS * WIDE + 8, 128), F32)],
        compiler_params=pltpu.CompilerParams(vmem_limit_bytes=VMEM_LIMIT // 2),
        cost_estimate=pl.CostEstimate(flops=10**8, bytes_accessed=10**6, transcendentals=0),
    )(kernel)


def weight_strips(top_rows, bottom_rows, left_cols, right_cols):
    def beside(first, last, axis):
        count = lax.axis_size(axis)
        up = [(i, (i + 1) % count) for i in range(count)]
        down = [(j, i) for i, j in up]
        return lax.ppermute(last, axis, up), lax.ppermute(first, axis, down)

    left, right = beside(left_cols, right_cols, "col")
    last = right.shape[0] - RAD
    top, bottom = beside(
        jnp.concatenate([top_rows, right[:RAD], left[:RAD]], axis=1),
        jnp.concatenate([bottom_rows, right[last:], left[last:]], axis=1),
        "row",
    )
    r, c = lax.axis_index("row"), lax.axis_index("col")
    inside = jnp.stack([r > 0, r < lax.axis_size("row") - 1, c > 0, c < lax.axis_size("col") - 1])
    return top, bottom, left, right, inside.astype(jnp.int32)


def spread(x_ref, left, right, out_ref, rows, cols):
    for b in range(cols // BLK + 1):
        if b == 0:
            piece = jnp.concatenate([left, x_ref[:, 0:RAD]], axis=1)
        elif b == cols // BLK:
            piece = jnp.concatenate([x_ref[:, cols - RAD : cols], right], axis=1)
        else:
            piece = x_ref[:, BLK * b - RAD : BLK * b + RAD]
        out_ref[pl.ds(b, rows, stride=PITCH), :] = jnp.concatenate([piece] * 4, axis=1)
    for b in range(cols // BLK + 1, PITCH):
        out_ref[pl.ds(b, rows, stride=PITCH), :] = jnp.zeros((rows, 128), F32)


def channel_weights(socs_ref):
    k = iota((1, 256), 1) // (2 * BLK)
    wv = jnp.zeros((1, 256), F32)
    for i in range(4):
        wv = jnp.where(k == i, socs_ref[i], wv)
    return wv


def windows(mask, s_ref, first, cols):
    count = mask.shape[0]
    for b in range(cols // BLK + 1):
        if b == 0:
            window = jnp.concatenate([mask[:, cols + BLK : cols + 2 * BLK], mask[:, 0:BLK]], axis=1)
        else:
            window = mask[:, BLK * (b - 1) : BLK * (b + 1)]
        s_ref[pl.ds(first * PITCH + b, count, stride=PITCH), :] = jnp.concatenate([window, window], axis=1)


def four_rows(s_ref, a_ref, start, end, step):
    first_half = iota((step, 128), 1) < 64
    for m in range(start, end, step):
        for h in range(2):
            even = s_ref[m + 2 * h * PITCH : m + 2 * h * PITCH + step, :]
            odd = s_ref[m + (2 * h + 1) * PITCH : m + (2 * h + 1) * PITCH + step, :]
            a_ref[m : m + step, 128 * h : 128 * h + 128] = jnp.where(first_half, even, odd).astype(BF16)


def correlate(a_ref, starts, count, table_ref):
    fields = None
    for g in range(AROWS // 4):
        parts = [a_ref[m + 4 * PITCH * g : m + 4 * PITCH * g + count, :] for m in starts]
        left = parts[0] if len(parts) == 1 else jnp.concatenate(parts, axis=0)
        right = table_ref[LEAD + 4 * g : LEAD + 4 * g + 4].reshape(8 * BLK, 256)
        term = jnp.dot(left, right, preferred_element_type=F32)
        fields = term if fields is None else fields + term
    return fields


def resist_and_gradient(fields, signed, wv, gs_ref, at):
    square = fields * fields * wv
    intensity = square[:, :128] + square[:, 128:]
    intensity = intensity + pltpu.roll(intensity, 64, 1)
    intensity = intensity + pltpu.roll(intensity, 32, 1)
    resist = 1.0 / (1.0 + jnp.exp(3.0 - intensity))
    slope = 2.0 * (jnp.abs(signed) * resist - jnp.maximum(signed, 0.0)) * resist * (1.0 - resist)
    for h in range(2):
        lanes = slice(128 * h, 128 * h + 128)
        value = (2.0 * wv[:, lanes]) * fields[:, lanes] * slope
        gs_ref[at : at + fields.shape[0], lanes] = value.astype(gs_ref.dtype)
    return resist


def imaging_kernel(
    inbox_ref, table_ref, signed_ref, left_ref, right_ref, socs_ref, inside_ref,
    loss_ref, edges_ref, gs_ref, mask_ref, s_ref, a_ref, sw_ref,
):
    rows, cols = signed_ref.shape
    halo = 2 * RAD
    tall = rows + 2 * halo
    words = [inbox_ref[:, 0, :].T, inbox_ref[:, 1, :].T]
    lower = [(x & 0xFFFF).astype(F32) * 0.25 for x in words]
    upper = [(x >> 16).astype(F32) * 0.25 for x in words]
    cell = iota((BLK, 128), 0).astype(F32).astype(BF16)
    cell_end = (iota((BLK, 128), 0) + 1).astype(F32).astype(BF16)

    def covers(group, at, first, count):
        low8, high8 = lower[group][at : at + CAP, :], upper[group][at : at + CAP, :]
        stacked = []
        for base in range(first, first + count, BLK):
            low = jnp.clip(low8 - float(base), 0.0, float(BLK))
            high = jnp.clip(high8 - float(base), 0.0, float(BLK))
            parts = []
            for rank in range(CAP):
                lo = jnp.broadcast_to(low[rank : rank + 1, :], (BLK, 128)).astype(BF16)
                hi = jnp.broadcast_to(high[rank : rank + 1, :], (BLK, 128)).astype(BF16)
                parts.append(jnp.maximum(jnp.minimum(hi, cell_end) - jnp.maximum(lo, cell), 0.0))
            stacked.append(jnp.concatenate(parts, axis=1))
        return stacked[0] if len(stacked) == 1 else jnp.concatenate(stacked, axis=0)

    row_span = {-1: (rows - halo, halo, 0), 0: (0, rows, halo), 1: (0, halo, halo + rows)}
    col_span = {-1: (cols - halo, halo, cols + halo), 0: (0, cols, 0), 1: (0, halo, cols)}
    for n, (dr, dc) in enumerate(NEIGHBOURS + [(0, 0)]):
        group, at = (1, 0) if n == 8 else (0, 16 * n)
        r_first, r_count, r_at = row_span[dr]
        c_first, c_count, c_at = col_span[dc]
        row_cover = covers(group, at + 8, r_first, r_count)
        col_cover = covers(group, at, c_first, c_count)
        part = dot_nt(row_cover, col_cover).astype(BF16).astype(F32)
        mask_ref[r_at : r_at + r_count, c_at : c_at + c_count] = part

    edges_ref[0:64, :] = mask_ref[0:64, :].astype(BF16)
    edges_ref[64:112, :] = mask_ref[tall - 48 : tall, :].astype(BF16)
    s_ref[...] = jnp.zeros(s_ref.shape, F32)
    windows(mask_ref[...], s_ref, 0, cols)
    four_rows(s_ref, a_ref, RAD * PITCH, (tall - RAD) * PITCH, 16 * PITCH)
    left = jnp.where(inside_ref[2] > 0, left_ref[...], 0.0)
    right = jnp.where(inside_ref[3] > 0, right_ref[...], 0.0)
    spread(signed_ref, left, right, sw_ref, rows, cols)

    wv = channel_weights(socs_ref)
    chunk = rows // 4 * PITCH
    block = iota((chunk, 128), 0) % PITCH
    co = iota((chunk, 128), 1) & (BLK - 1)
    own = ((block > 0) | (co >= RAD)) & ((block < cols // BLK) | (co < RAD)) & (block <= cols // BLK)
    total = jnp.zeros((1, 128), F32)
    for k in range(4):
        m = k * chunk
        fields = correlate(a_ref, [RAD * PITCH + m], chunk, table_ref)
        signed = sw_ref[m : m + chunk, :]
        resist = resist_and_gradient(fields, signed, wv, gs_ref, m)
        miss = resist - jnp.where(signed > 0.0, 1.0, 0.0)
        part = jnp.where(own, jnp.abs(signed), 0.0) * miss * miss
        total = total + jnp.sum(part, axis=0, keepdims=True)
    total = 0.25 * jnp.sum(total, axis=1, keepdims=True)
    loss_ref[...] = jnp.broadcast_to(total, loss_ref.shape)


def imaging(inbox, table, signed, left, right, socs_weight, inside, devices):
    rows, cols = signed.shape
    tall = rows + 4 * RAD
    return pl.pallas_call(
        imaging_kernel,
        out_shape=(
            pltpu.VMEM((devices, 1, 128), F32),
            pltpu.VMEM((112, cols + 128), BF16),
            pltpu.VMEM((rows * PITCH, 256), BF16),
        ),
        in_specs=[WHOLE] * 5 + [SMALL] * 2,
        scratch_shapes=[
            pltpu.VMEM((tall, cols + 128), F32),
            pltpu.VMEM(((tall + 4) * PITCH, 128), F32),
            pltpu.VMEM((tall * PITCH, 256), BF16),
            pltpu.VMEM((rows * PITCH, 128), F32),
        ],
        compiler_params=pltpu.CompilerParams(vmem_limit_bytes=VMEM_LIMIT),
        cost_estimate=pl.CostEstimate(flops=4 * 10**9, bytes_accessed=8 * 10**6, transcendentals=10**6),
    )(inbox, table, signed, left, right, socs_weight, inside)


def adjoint_kernel(
    edges_ref, table_ref, gs_ref, top_ref, bottom_ref, socs_ref, inside_ref,
    out_ref, s_ref, a_ref, x_ref, sw_ref, gw_ref, g_ref, acc_ref, tile_ref,
):
    rows, cols = out_ref.shape
    ext = rows + 2 * RAD
    x_ref[0:RAD, :] = jnp.where(inside_ref[0] > 0, top_ref[...], 0.0)
    x_ref[RAD : 2 * RAD, :] = jnp.where(inside_ref[1] > 0, bottom_ref[...], 0.0)
    left = jnp.where(inside_ref[2] > 0, x_ref[:, cols + RAD : cols + 2 * RAD], 0.0)
    right = jnp.where(inside_ref[3] > 0, x_ref[:, cols : cols + RAD], 0.0)
    spread(x_ref, left, right, sw_ref, 2 * RAD, cols)
    s_ref[...] = jnp.zeros(s_ref.shape, F32)
    windows(edges_ref[0:64, :].astype(F32), s_ref, 0, cols)
    windows(edges_ref[64:112, :].astype(F32), s_ref, 64, cols)
    four_rows(s_ref, a_ref, 0, 48 * PITCH, 16 * PITCH)
    four_rows(s_ref, a_ref, 64 * PITCH, 112 * PITCH, 16 * PITCH)
    fields = correlate(a_ref, [0, 64 * PITCH], RAD * PITCH, table_ref)
    resist_and_gradient(fields, sw_ref[...], channel_weights(socs_ref), gw_ref, 0)
    gw_ref[2 * RAD * PITCH :, :] = gs_ref[...].astype(F32)

    for r in range(ext):
        for s in range(2):
            if r < RAD:
                row = r
            elif r >= RAD + rows:
                row = r - rows
            else:
                row = r + RAD
            at = row * PITCH + s
            g_ref[s, r % 8, r // 8] = gw_ref[at : at + 16, :].astype(BF16)

    total = jnp.zeros((256, 256), F32)
    for i in range(40):
        for s in range(2):
            fields = g_ref[s, i % 8, i // 8 : i // 8 + 16].reshape(256, 256)
            taps = table_ref[39 - i : 47 - i, BLK * (1 - s) : BLK * (2 - s), :].reshape(256, 256)
            total = total + dot_nt(fields, taps)
    for h in range(2):
        acc_ref[h] = total[:, 128 * h : 128 * h + 128]
    for q in range(cols // 128):
        for h in range(2):
            per_block = [acc_ref[h, pl.ds(4 * q + j, 16, stride=16), :] for j in range(4)]
            for j in range(4):
                pieces = [x[:, BLK * j : BLK * j + BLK] for x in per_block]
                tile_ref[q, pl.ds(4 * h + j, 16, stride=8), :] = jnp.concatenate(pieces, axis=1)
        out_ref[:, 128 * q : 128 * q + 128] = tile_ref[q]


def adjoint(edges, table, gs, top, bottom, socs_weight, inside, rows, cols):
    ext = rows + 2 * RAD
    return pl.pallas_call(
        adjoint_kernel,
        out_shape=jax.ShapeDtypeStruct((rows, cols), F32),
        in_specs=[WHOLE] * 5 + [SMALL] * 2,
        scratch_shapes=[
            pltpu.VMEM((116 * PITCH, 128), F32),
            pltpu.VMEM((112 * PITCH, 256), BF16),
            pltpu.VMEM((2 * RAD, cols + 2 * RAD), F32),
            pltpu.VMEM((2 * RAD * PITCH, 128), F32),
            pltpu.VMEM((ext * PITCH, 256), F32),
            pltpu.VMEM((2, 8, ext // 8, 16, 256), BF16),
            pltpu.VMEM((2, 256, 128), F32),
            pltpu.VMEM((cols // 128, rows, 128), F32),
        ],
        compiler_params=pltpu.CompilerParams(vmem_limit_bytes=VMEM_LIMIT),
        cost_estimate=pl.CostEstimate(flops=4 * 10**9, bytes_accessed=10**7, transcendentals=0),
    )(edges, table, gs, top, bottom, socs_weight, inside)


def shards(rects, owner, counts, target, loss_weight, kernel, socs_weight):
    row_devices = lax.axis_size("row")
    col_devices = lax.axis_size("col")
    devices = row_devices * col_devices
    rows, cols = target.shape
    outbox, signed, *strips = make_outbox(rects, owner, counts, target, loss_weight, devices, col_devices)
    inbox = lax.all_to_all(outbox, ("row", "col"), split_axis=0, concat_axis=0, tiled=True)
    table = make_tables(kernel)
    top, bottom, left, right, inside = weight_strips(*strips)
    local, edges, gs = imaging(inbox, table, signed, left, right, socs_weight, inside, devices)
    losses = lax.all_to_all(local, ("row", "col"), split_axis=0, concat_axis=0, tiled=True)
    mask_grad = adjoint(edges, table, gs, top, bottom, socs_weight, inside, rows, cols)
    window_area = rows * row_devices * cols * col_devices
    return (mask_grad, (jnp.sum(losses[:, 0, 0]) / window_area).reshape(1))


def solution(mesh):
    placed = (
        P(None, ("row", "col")),
        P(("row", "col")),
        P(("row", "col")),
        P("row", "col"),
        P("row", "col"),
        P(),
        P(),
    )
    return jax.shard_map(
        shards, mesh=mesh, in_specs=placed, out_specs=(P("row", "col"), P()), check_vma=False
    )
```

```python
import jax
import jax.numpy as jnp
from jax import lax
from jax.experimental import pallas as pl
from jax.experimental.pallas import tpu as pltpu
from jax.sharding import PartitionSpec as P

RAD = 16
CAP = 8
KS = 33
BLK = 32
GROUP = 8
WIDE = 2 * BLK + 1
PITCH = 18
NEIGHBOURS = [(dr, dc) for dr in (-1, 0, 1) for dc in (-1, 0, 1) if (dr, dc) != (0, 0)]
F32 = jnp.float32
BF16 = jnp.bfloat16
VMEM_LIMIT = 32 * 1024 * 1024


def dot_nt(a, b):
    return lax.dot_general(a, b, (((1,), (1,)), ((), ())), preferred_element_type=F32)


def iota(shape, dim):
    return lax.broadcasted_iota(jnp.int32, shape, dim)


def outbox_kernel(
    tile_cols, counts_ref, rects_ref, owner_ref, target_ref, weight_ref,
    out_ref, signed_ref, top_ref, bottom_ref, left_ref, right_ref,
    pad_ref, target_buf, weight_buf, sems,
):
    rows, cols = signed_ref.shape
    load_target = pltpu.make_async_copy(target_ref, target_buf, sems.at[0])
    load_weight = pltpu.make_async_copy(weight_ref, weight_buf, sems.at[1])
    load_target.start()
    load_weight.start()
    slots = owner_ref.shape[1]
    tiles = out_ref.shape[0]
    live = iota((1, slots), 1) < counts_ref[0]
    own = jnp.where(live, owner_ref[...], -1)
    hit = iota((tiles, slots), 0) == own
    hits = jnp.where(hit, 1.0, 0.0).astype(BF16)
    before = jnp.where(iota((slots, slots), 0) < iota((slots, slots), 1), 1.0, 0.0).astype(BF16)
    earlier = jnp.dot(hits, before, preferred_element_type=F32)
    rank = jnp.sum(jnp.where(hit, earlier, 0.0), axis=0, keepdims=True).astype(jnp.int32)
    row = iota((16, slots), 0)
    chosen = rank == (row & 7)
    vertical = (row & 8) == 8

    def placed(first, second):
        value = jnp.where(vertical, second, first)
        value = jnp.where(chosen, value, 0)
        high = (value >> 4).astype(F32).astype(BF16)
        low = (value & 15).astype(F32).astype(BF16)
        return (16.0 * dot_nt(hits, high) + dot_nt(hits, low)).astype(jnp.int32)

    lower = placed(rects_ref[0:1, :], rects_ref[2:3, :])
    upper = placed(rects_ref[1:2, :], rects_ref[3:4, :])
    word = lower + (upper << 16)
    word = jnp.concatenate([word] * 8, axis=1)
    pad_ref[...] = jnp.zeros(pad_ref.shape, jnp.int32)
    pad_ref[24 : 24 + tiles, :] = word
    column = iota((tiles, 128), 0) % tile_cols
    group = iota((tiles, 128), 1) >> 4
    result = jnp.zeros((tiles, 128), jnp.int32)
    for n, (dr, dc) in enumerate(NEIGHBOURS):
        start = 24 + dr * tile_cols + dc
        inside = (column + dc >= 0) & (column + dc < tile_cols) & (group == n)
        result = jnp.where(inside, pad_ref[start : start + tiles, :], result)
    out_ref[:, 0, :] = result
    out_ref[:, 1, :] = word
    load_target.wait()
    load_weight.wait()
    signed_ref[...] = jnp.where(target_buf[...] > 0, weight_buf[...], -weight_buf[...])
    top_ref[...] = signed_ref[0:RAD, :]
    bottom_ref[...] = signed_ref[rows - RAD : rows, :]
    left_ref[...] = signed_ref[:, 0:RAD]
    right_ref[...] = signed_ref[:, cols - RAD : cols]


SMALL = pl.BlockSpec(memory_space=pltpu.SMEM)
WHOLE = pl.BlockSpec(memory_space=pltpu.VMEM)
ANYWHERE = pl.BlockSpec(memory_space=pl.ANY)


def make_outbox(rects, owner, counts, target, weight, tiles, tile_cols):
    slots = owner.shape[0]
    rows, cols = target.shape
    return pl.pallas_call(
        lambda *refs: outbox_kernel(tile_cols, *refs),
        out_shape=(
            pltpu.VMEM((tiles, 2, 128), jnp.int32),
            pltpu.VMEM((rows, cols), F32),
            pltpu.VMEM((RAD, cols), F32),
            pltpu.VMEM((RAD, cols), F32),
            pltpu.VMEM((rows, RAD), F32),
            pltpu.VMEM((rows, RAD), F32),
        ),
        in_specs=[SMALL, WHOLE, WHOLE, ANYWHERE, ANYWHERE],
        scratch_shapes=[
            pltpu.VMEM((tiles + 48, 128), jnp.int32),
            pltpu.VMEM((rows, cols), jnp.int32),
            pltpu.VMEM((rows, cols), F32),
            pltpu.SemaphoreType.DMA((2,)),
        ],
        cost_estimate=pl.CostEstimate(flops=10**8, bytes_accessed=10**6, transcendentals=0),
    )(counts, rects, owner.reshape(1, slots), target, weight)


def tables_kernel(kernel_ref, table_ref, wide_ref):
    channels = kernel_ref.shape[1]
    lanes = channels * BLK
    tap, lane = iota((KS, lanes), 0), iota((KS, lanes), 1) % BLK
    flat = kernel_ref[...].astype(F32).reshape(KS * channels, KS).astype(BF16)
    mine = iota((KS, channels, lanes), 1) == iota((KS, channels, lanes), 2) // BLK

    def by_lane(picked):
        every = jnp.dot(flat, jnp.where(picked, 1.0, 0.0).astype(BF16), preferred_element_type=F32)
        return jnp.sum(jnp.where(mine, every.reshape(KS, channels, lanes), 0.0), axis=1)

    taps = by_lane(tap == KS - 1 - lane)
    edge = by_lane(tap == 0)
    co = iota((KS, 128), 1) % BLK
    for p in range(BLK):
        for h in range(lanes // 128):
            mine = taps[:, 128 * h : 128 * h + 128]
            ends = edge[:, 128 * h : 128 * h + 128]
            near = pltpu.roll(mine, p, 1) if p else mine
            far = pltpu.roll(mine, p + 128 - BLK, 1)
            far = jnp.where(co < p, far, jnp.where(co == p, ends, 0.0))
            wide_ref[h, pl.ds(p, KS, stride=WIDE), :] = far
            wide_ref[h, pl.ds(BLK + p, KS, stride=WIDE), :] = jnp.where(co >= p, near, 0.0)
    for a in range(KS):
        for h in range(lanes // 128):
            table_ref[a, :, 128 * h : 128 * h + 128] = wide_ref[h, a * WIDE : a * WIDE + 2 * BLK, :].astype(BF16)


def make_tables(kernel):
    lanes = kernel.shape[0] * BLK
    return pl.pallas_call(
        tables_kernel,
        out_shape=pltpu.VMEM((KS, 2 * BLK, lanes), BF16),
        in_specs=[WHOLE],
        scratch_shapes=[pltpu.VMEM((lanes // 128, KS * WIDE + 8, 128), F32)],
        compiler_params=pltpu.CompilerParams(vmem_limit_bytes=VMEM_LIMIT // 2),
        cost_estimate=pl.CostEstimate(flops=10**10, bytes_accessed=10**6, transcendentals=0),
    )(kernel.transpose(1, 0, 2))


def weight_strips(top_rows, bottom_rows, left_cols, right_cols):
    def beside(first, last, axis):
        count = lax.axis_size(axis)
        up = [(i, (i + 1) % count) for i in range(count)]
        down = [(j, i) for i, j in up]
        return lax.ppermute(last, axis, up), lax.ppermute(first, axis, down)

    left, right = beside(left_cols, right_cols, "col")
    last = right.shape[0] - RAD
    top, bottom = beside(
        jnp.concatenate([top_rows, right[:RAD], left[:RAD]], axis=1),
        jnp.concatenate([bottom_rows, right[last:], left[last:]], axis=1),
        "row",
    )
    r, c = lax.axis_index("row"), lax.axis_index("col")
    inside = jnp.stack([r > 0, r < lax.axis_size("row") - 1, c > 0, c < lax.axis_size("col") - 1])
    return top, bottom, left, right, inside.astype(jnp.int32)


def spread(x_ref, left, right, out_ref, rows, cols):
    for b in range(cols // BLK + 1):
        if b == 0:
            piece = jnp.concatenate([left, x_ref[:, 0:RAD]], axis=1)
        elif b == cols // BLK:
            piece = jnp.concatenate([x_ref[:, cols - RAD : cols], right], axis=1)
        else:
            piece = x_ref[:, BLK * b - RAD : BLK * b + RAD]
        out_ref[pl.ds(b, rows, stride=PITCH), :] = jnp.concatenate([piece] * 4, axis=1)
    for b in range(cols // BLK + 1, PITCH):
        out_ref[pl.ds(b, rows, stride=PITCH), :] = jnp.zeros((rows, 128), F32)


def channel_weights(socs_ref):
    k = iota((1, 256), 1) // (2 * BLK)
    wv = jnp.zeros((1, 256), F32)
    for i in range(4):
        wv = jnp.where(k == i, socs_ref[i], wv)
    return wv


def windows(mask, s_ref, first, cols):
    count = mask.shape[0]
    for b in range(cols // BLK + 1):
        if b == 0:
            window = jnp.concatenate([mask[:, cols + BLK : cols + 2 * BLK], mask[:, 0:BLK]], axis=1)
        else:
            window = mask[:, BLK * (b - 1) : BLK * (b + 1)]
        s_ref[pl.ds(first * PITCH + b, count, stride=PITCH), :] = jnp.concatenate([window, window], axis=1)
    for b in range(cols // BLK + 1, PITCH):
        s_ref[pl.ds(first * PITCH + b, count, stride=PITCH), :] = jnp.zeros((count, 128), F32)


def group_rows(s_ref, a_ref, start, end, step):
    first_half = iota((step, 128), 1) < 64
    for m in range(start, end, step):
        for h in range(GROUP // 2):
            even = s_ref[m + 2 * h * PITCH : m + 2 * h * PITCH + step, :]
            odd = s_ref[m + (2 * h + 1) * PITCH : m + (2 * h + 1) * PITCH + step, :]
            a_ref[m : m + step, 128 * h : 128 * h + 128] = jnp.where(first_half, even, odd).astype(BF16)


def correlate(a_ref, starts, count, table_ref):
    fields = None
    for g in range(0, KS, GROUP):
        taken = min(GROUP, KS - g)
        right = table_ref[g : g + taken].reshape(taken * 2 * BLK, 256)
        if taken % 2:
            right = jnp.concatenate([right, jnp.zeros((2 * BLK, 256), BF16)], axis=0)
        lanes = slice(0, right.shape[0])
        parts = [a_ref[m + PITCH * g : m + PITCH * g + count, lanes] for m in starts]
        left = parts[0] if len(parts) == 1 else jnp.concatenate(parts, axis=0)
        term = jnp.dot(left, right, preferred_element_type=F32)
        fields = term if fields is None else fields + term
    return fields


def resist_and_gradient(fields, signed, wv, gs_ref, at):
    square = fields * fields * wv
    intensity = square[:, :128] + square[:, 128:]
    intensity = intensity + pltpu.roll(intensity, 64, 1)
    intensity = intensity + pltpu.roll(intensity, 32, 1)
    resist = 1.0 / (1.0 + jnp.exp(3.0 - intensity))
    slope = 2.0 * (jnp.abs(signed) * resist - jnp.maximum(signed, 0.0)) * resist * (1.0 - resist)
    for h in range(2):
        lanes = slice(128 * h, 128 * h + 128)
        value = (2.0 * wv[:, lanes]) * fields[:, lanes] * slope
        gs_ref[at : at + fields.shape[0], lanes] = value.astype(gs_ref.dtype)
    return resist


def imaging_kernel(
    inbox_ref, table_ref, signed_ref, left_ref, right_ref, socs_ref, inside_ref,
    loss_ref, edges_ref, gs_ref, mask_ref, s_ref, a_ref, sw_ref,
):
    rows, cols = signed_ref.shape
    halo = 2 * RAD
    tall = rows + 2 * halo
    words = [inbox_ref[:, 0, :].T, inbox_ref[:, 1, :].T]
    lower = [(x & 0xFFFF).astype(F32) * 0.25 for x in words]
    upper = [(x >> 16).astype(F32) * 0.25 for x in words]
    cell = iota((BLK, 128), 0).astype(F32).astype(BF16)
    cell_end = (iota((BLK, 128), 0) + 1).astype(F32).astype(BF16)

    def covers(group, at, first, count):
        low8, high8 = lower[group][at : at + CAP, :], upper[group][at : at + CAP, :]
        stacked = []
        for base in range(first, first + count, BLK):
            low = jnp.clip(low8 - float(base), 0.0, float(BLK))
            high = jnp.clip(high8 - float(base), 0.0, float(BLK))
            parts = []
            for rank in range(CAP):
                lo = jnp.broadcast_to(low[rank : rank + 1, :], (BLK, 128)).astype(BF16)
                hi = jnp.broadcast_to(high[rank : rank + 1, :], (BLK, 128)).astype(BF16)
                parts.append(jnp.maximum(jnp.minimum(hi, cell_end) - jnp.maximum(lo, cell), 0.0))
            stacked.append(jnp.concatenate(parts, axis=1))
        return stacked[0] if len(stacked) == 1 else jnp.concatenate(stacked, axis=0)

    row_span = {-1: (rows - halo, halo, 0), 0: (0, rows, halo), 1: (0, halo, halo + rows)}
    col_span = {-1: (cols - halo, halo, cols + halo), 0: (0, cols, 0), 1: (0, halo, cols)}
    for n, (dr, dc) in enumerate(NEIGHBOURS + [(0, 0)]):
        group, at = (1, 0) if n == 8 else (0, 16 * n)
        r_first, r_count, r_at = row_span[dr]
        c_first, c_count, c_at = col_span[dc]
        row_cover = covers(group, at + 8, r_first, r_count)
        col_cover = covers(group, at, c_first, c_count)
        part = dot_nt(row_cover, col_cover).astype(BF16).astype(F32)
        mask_ref[r_at : r_at + r_count, c_at : c_at + c_count] = part

    edges_ref[0:64, :] = mask_ref[0:64, :].astype(BF16)
    edges_ref[64:112, :] = mask_ref[tall - 48 : tall, :].astype(BF16)
    s_ref[tall * PITCH :, :] = jnp.zeros((8 * PITCH, 128), F32)
    windows(mask_ref[...], s_ref, 0, cols)
    group_rows(s_ref, a_ref, RAD * PITCH, (tall - RAD) * PITCH, 16 * PITCH)
    left = jnp.where(inside_ref[2] > 0, left_ref[...], 0.0)
    right = jnp.where(inside_ref[3] > 0, right_ref[...], 0.0)
    spread(signed_ref, left, right, sw_ref, rows, cols)

    wv = channel_weights(socs_ref)
    chunk = rows // 4 * PITCH
    block = iota((chunk, 128), 0) % PITCH
    co = iota((chunk, 128), 1) & (BLK - 1)
    own = ((block > 0) | (co >= RAD)) & ((block < cols // BLK) | (co < RAD)) & (block <= cols // BLK)
    total = jnp.zeros((1, 128), F32)
    for k in range(4):
        m = k * chunk
        fields = correlate(a_ref, [RAD * PITCH + m], chunk, table_ref)
        signed = sw_ref[m : m + chunk, :]
        resist = resist_and_gradient(fields, signed, wv, gs_ref, m)
        miss = resist - jnp.where(signed > 0.0, 1.0, 0.0)
        part = jnp.where(own, jnp.abs(signed), 0.0) * miss * miss
        total = total + jnp.sum(part, axis=0, keepdims=True)
    total = 0.25 * jnp.sum(total, axis=1, keepdims=True)
    loss_ref[...] = jnp.broadcast_to(total, loss_ref.shape)


def imaging(inbox, table, signed, left, right, socs_weight, inside, devices):
    rows, cols = signed.shape
    tall = rows + 4 * RAD
    return pl.pallas_call(
        imaging_kernel,
        out_shape=(
            pltpu.VMEM((devices, 1, 128), F32),
            pltpu.VMEM((112, cols + 128), BF16),
            pltpu.VMEM((rows * PITCH, 256), BF16),
        ),
        in_specs=[WHOLE] * 5 + [SMALL] * 2,
        scratch_shapes=[
            pltpu.VMEM((tall, cols + 128), F32),
            pltpu.VMEM(((tall + 8) * PITCH, 128), F32),
            pltpu.VMEM((tall * PITCH, 64 * GROUP), BF16),
            pltpu.VMEM((rows * PITCH, 128), F32),
        ],
        compiler_params=pltpu.CompilerParams(vmem_limit_bytes=VMEM_LIMIT),
        cost_estimate=pl.CostEstimate(flops=4 * 10**9, bytes_accessed=8 * 10**6, transcendentals=10**6),
    )(inbox, table, signed, left, right, socs_weight, inside)


def adjoint_taps(table_ref, start, at):
    first, last = max(start, 0), min(start + 8, KS)
    pieces = [table_ref[first:last, at : at + BLK, :].reshape((last - first) * BLK, 256)]
    if first > start:
        pieces.insert(0, jnp.zeros(((first - start) * BLK, 256), BF16))
    if last < start + 8:
        pieces.append(jnp.zeros(((start + 8 - last) * BLK, 256), BF16))
    return pieces[0] if len(pieces) == 1 else jnp.concatenate(pieces, axis=0)


def adjoint_kernel(
    edges_ref, table_ref, gs_ref, top_ref, bottom_ref, socs_ref, inside_ref,
    out_ref, s_ref, a_ref, x_ref, sw_ref, gw_ref, g_ref, acc_ref, tile_ref,
):
    rows, cols = out_ref.shape
    ext = rows + 2 * RAD
    x_ref[0:RAD, :] = jnp.where(inside_ref[0] > 0, top_ref[...], 0.0)
    x_ref[RAD : 2 * RAD, :] = jnp.where(inside_ref[1] > 0, bottom_ref[...], 0.0)
    left = jnp.where(inside_ref[2] > 0, x_ref[:, cols + RAD : cols + 2 * RAD], 0.0)
    right = jnp.where(inside_ref[3] > 0, x_ref[:, cols : cols + RAD], 0.0)
    spread(x_ref, left, right, sw_ref, 2 * RAD, cols)
    s_ref[112 * PITCH :, :] = jnp.zeros((8 * PITCH, 128), F32)
    windows(edges_ref[0:64, :].astype(F32), s_ref, 0, cols)
    windows(edges_ref[64:112, :].astype(F32), s_ref, 64, cols)
    group_rows(s_ref, a_ref, 0, 48 * PITCH, 16 * PITCH)
    group_rows(s_ref, a_ref, 64 * PITCH, 112 * PITCH, 16 * PITCH)
    fields = correlate(a_ref, [0, 64 * PITCH], RAD * PITCH, table_ref)
    resist_and_gradient(fields, sw_ref[...], channel_weights(socs_ref), gw_ref, 0)
    gw_ref[2 * RAD * PITCH :, :] = gs_ref[...].astype(F32)

    for r in range(ext):
        for s in range(2):
            if r < RAD:
                row = r
            elif r >= RAD + rows:
                row = r - rows
            else:
                row = r + RAD
            at = row * PITCH + s
            g_ref[s, r % 8, r // 8] = gw_ref[at : at + 16, :].astype(BF16)

    total = jnp.zeros((256, 256), F32)
    for i in range(40):
        for s in range(2):
            fields = g_ref[s, i % 8, i // 8 : i // 8 + 16].reshape(256, 256)
            total = total + dot_nt(fields, adjoint_taps(table_ref, KS - 1 - i, BLK * (1 - s)))
    for h in range(2):
        acc_ref[h] = total[:, 128 * h : 128 * h + 128]
    for q in range(cols // 128):
        for h in range(2):
            per_block = [acc_ref[h, pl.ds(4 * q + j, 16, stride=16), :] for j in range(4)]
            for j in range(4):
                pieces = [x[:, BLK * j : BLK * j + BLK] for x in per_block]
                tile_ref[q, pl.ds(4 * h + j, 16, stride=8), :] = jnp.concatenate(pieces, axis=1)
        out_ref[:, 128 * q : 128 * q + 128] = tile_ref[q]


def adjoint(edges, table, gs, top, bottom, socs_weight, inside, rows, cols):
    ext = rows + 2 * RAD
    return pl.pallas_call(
        adjoint_kernel,
        out_shape=jax.ShapeDtypeStruct((rows, cols), F32),
        in_specs=[WHOLE] * 5 + [SMALL] * 2,
        scratch_shapes=[
            pltpu.VMEM((120 * PITCH, 128), F32),
            pltpu.VMEM((112 * PITCH, 64 * GROUP), BF16),
            pltpu.VMEM((2 * RAD, cols + 2 * RAD), F32),
            pltpu.VMEM((2 * RAD * PITCH, 128), F32),
            pltpu.VMEM((ext * PITCH, 256), F32),
            pltpu.VMEM((2, 8, ext // 8, 16, 256), BF16),
            pltpu.VMEM((2, 256, 128), F32),
            pltpu.VMEM((cols // 128, rows, 128), F32),
        ],
        compiler_params=pltpu.CompilerParams(vmem_limit_bytes=VMEM_LIMIT),
        cost_estimate=pl.CostEstimate(flops=4 * 10**9, bytes_accessed=10**7, transcendentals=0),
    )(edges, table, gs, top, bottom, socs_weight, inside)


def shards(rects, owner, counts, target, loss_weight, kernel, socs_weight):
    row_devices = lax.axis_size("row")
    col_devices = lax.axis_size("col")
    devices = row_devices * col_devices
    rows, cols = target.shape
    outbox, signed, *strips = make_outbox(rects, owner, counts, target, loss_weight, devices, col_devices)
    inbox = lax.all_to_all(outbox, ("row", "col"), split_axis=0, concat_axis=0, tiled=True)
    table = make_tables(kernel)
    top, bottom, left, right, inside = weight_strips(*strips)
    local, edges, gs = imaging(inbox, table, signed, left, right, socs_weight, inside, devices)
    losses = lax.all_to_all(local, ("row", "col"), split_axis=0, concat_axis=0, tiled=True)
    mask_grad = adjoint(edges, table, gs, top, bottom, socs_weight, inside, rows, cols)
    window_area = rows * row_devices * cols * col_devices
    return (mask_grad, (jnp.sum(losses[:, 0, 0]) / window_area).reshape(1))


def solution(mesh):
    placed = (
        P(None, ("row", "col")),
        P(("row", "col")),
        P(("row", "col")),
        P("row", "col"),
        P("row", "col"),
        P(),
        P(),
    )
    return jax.shard_map(
        shards, mesh=mesh, in_specs=placed, out_specs=(P("row", "col"), P()), check_vma=False
    )
```

```python
import jax
import jax.numpy as jnp
from jax import lax
from jax.experimental import pallas as pl
from jax.experimental.pallas import tpu as pltpu
from jax.sharding import PartitionSpec as P

RAD = 16
CAP = 8
KS = 33
BLK = 32
GROUP = 8
WIDE = 2 * BLK + 1
PITCH = 18
NEIGHBOURS = [(dr, dc) for dr in (-1, 0, 1) for dc in (-1, 0, 1) if (dr, dc) != (0, 0)]
F32 = jnp.float32
BF16 = jnp.bfloat16
VMEM_LIMIT = 32 * 1024 * 1024


def dot_nt(a, b):
    return lax.dot_general(a, b, (((1,), (1,)), ((), ())), preferred_element_type=F32)


def iota(shape, dim):
    return lax.broadcasted_iota(jnp.int32, shape, dim)


def outbox_kernel(
    tile_cols, counts_ref, rects_ref, owner_ref, target_ref, weight_ref,
    out_ref, signed_ref, top_ref, bottom_ref, left_ref, right_ref,
    pad_ref, target_buf, weight_buf, sems,
):
    rows, cols = signed_ref.shape
    load_target = pltpu.make_async_copy(target_ref, target_buf, sems.at[0])
    load_weight = pltpu.make_async_copy(weight_ref, weight_buf, sems.at[1])
    load_target.start()
    load_weight.start()
    slots = owner_ref.shape[1]
    tiles = out_ref.shape[0]
    live = iota((1, slots), 1) < counts_ref[0]
    own = jnp.where(live, owner_ref[...], -1)
    hit = iota((tiles, slots), 0) == own
    hits = jnp.where(hit, 1.0, 0.0).astype(BF16)
    before = jnp.where(iota((slots, slots), 0) < iota((slots, slots), 1), 1.0, 0.0).astype(BF16)
    earlier = jnp.dot(hits, before, preferred_element_type=F32)
    rank = jnp.sum(jnp.where(hit, earlier, 0.0), axis=0, keepdims=True).astype(jnp.int32)
    row = iota((16, slots), 0)
    chosen = rank == (row & 7)
    vertical = (row & 8) == 8

    def placed(first, second):
        value = jnp.where(vertical, second, first)
        value = jnp.where(chosen, value, 0)
        high = (value >> 4).astype(F32).astype(BF16)
        low = (value & 15).astype(F32).astype(BF16)
        return (16.0 * dot_nt(hits, high) + dot_nt(hits, low)).astype(jnp.int32)

    lower = placed(rects_ref[0:1, :], rects_ref[2:3, :])
    upper = placed(rects_ref[1:2, :], rects_ref[3:4, :])
    word = lower + (upper << 16)
    word = jnp.concatenate([word] * 8, axis=1)
    pad_ref[...] = jnp.zeros(pad_ref.shape, jnp.int32)
    pad_ref[24 : 24 + tiles, :] = word
    column = iota((tiles, 128), 0) % tile_cols
    group = iota((tiles, 128), 1) >> 4
    result = jnp.zeros((tiles, 128), jnp.int32)
    for n, (dr, dc) in enumerate(NEIGHBOURS):
        start = 24 + dr * tile_cols + dc
        inside = (column + dc >= 0) & (column + dc < tile_cols) & (group == n)
        result = jnp.where(inside, pad_ref[start : start + tiles, :], result)
    out_ref[:, 0, :] = result
    out_ref[:, 1, :] = word
    load_target.wait()
    load_weight.wait()
    signed_ref[...] = jnp.where(target_buf[...] > 0, weight_buf[...], -weight_buf[...])
    top_ref[...] = signed_ref[0:RAD, :]
    bottom_ref[...] = signed_ref[rows - RAD : rows, :]
    left_ref[...] = signed_ref[:, 0:RAD]
    right_ref[...] = signed_ref[:, cols - RAD : cols]


SMALL = pl.BlockSpec(memory_space=pltpu.SMEM)
WHOLE = pl.BlockSpec(memory_space=pltpu.VMEM)
ANYWHERE = pl.BlockSpec(memory_space=pl.ANY)


def make_outbox(rects, owner, counts, target, weight, tiles, tile_cols):
    slots = owner.shape[0]
    rows, cols = target.shape
    return pl.pallas_call(
        lambda *refs: outbox_kernel(tile_cols, *refs),
        out_shape=(
            pltpu.VMEM((tiles, 2, 128), jnp.int32),
            pltpu.VMEM((rows, cols), F32),
            pltpu.VMEM((RAD, cols), F32),
            pltpu.VMEM((RAD, cols), F32),
            pltpu.VMEM((rows, RAD), F32),
            pltpu.VMEM((rows, RAD), F32),
        ),
        in_specs=[SMALL, WHOLE, WHOLE, ANYWHERE, ANYWHERE],
        scratch_shapes=[
            pltpu.VMEM((tiles + 48, 128), jnp.int32),
            pltpu.VMEM((rows, cols), jnp.int32),
            pltpu.VMEM((rows, cols), F32),
            pltpu.SemaphoreType.DMA((2,)),
        ],
        cost_estimate=pl.CostEstimate(flops=10**8, bytes_accessed=10**6, transcendentals=0),
    )(counts, rects, owner.reshape(1, slots), target, weight)


def tables_kernel(kernel_ref, table_ref, wide_ref):
    channels = kernel_ref.shape[1]
    lanes = channels * BLK
    tap, lane = iota((KS, lanes), 0), iota((KS, lanes), 1) % BLK
    flat = kernel_ref[...].astype(F32).reshape(KS * channels, KS).astype(BF16)
    mine = iota((KS, channels, lanes), 1) == iota((KS, channels, lanes), 2) // BLK

    def by_lane(picked):
        every = jnp.dot(flat, jnp.where(picked, 1.0, 0.0).astype(BF16), preferred_element_type=F32)
        return jnp.sum(jnp.where(mine, every.reshape(KS, channels, lanes), 0.0), axis=1)

    taps = by_lane(tap == KS - 1 - lane)
    edge = by_lane(tap == 0)
    co = iota((KS, 128), 1) % BLK
    for p in range(BLK):
        for h in range(lanes // 128):
            mine = taps[:, 128 * h : 128 * h + 128]
            ends = edge[:, 128 * h : 128 * h + 128]
            near = pltpu.roll(mine, p, 1) if p else mine
            far = pltpu.roll(mine, p + 128 - BLK, 1)
            far = jnp.where(co < p, far, jnp.where(co == p, ends, 0.0))
            wide_ref[h, pl.ds(p, KS, stride=WIDE), :] = far
            wide_ref[h, pl.ds(BLK + p, KS, stride=WIDE), :] = jnp.where(co >= p, near, 0.0)
    for a in range(KS):
        for h in range(lanes // 128):
            table_ref[a, :, 128 * h : 128 * h + 128] = wide_ref[h, a * WIDE : a * WIDE + 2 * BLK, :].astype(BF16)


def make_tables(kernel):
    lanes = kernel.shape[0] * BLK
    return pl.pallas_call(
        tables_kernel,
        out_shape=pltpu.VMEM((KS, 2 * BLK, lanes), BF16),
        in_specs=[WHOLE],
        scratch_shapes=[pltpu.VMEM((lanes // 128, KS * WIDE + 8, 128), F32)],
        compiler_params=pltpu.CompilerParams(vmem_limit_bytes=VMEM_LIMIT // 2),
        cost_estimate=pl.CostEstimate(flops=10**10, bytes_accessed=10**6, transcendentals=0),
    )(kernel.transpose(1, 0, 2))


def weight_strips(top_rows, bottom_rows, left_cols, right_cols):
    def beside(first, last, axis):
        count = lax.axis_size(axis)
        up = [(i, (i + 1) % count) for i in range(count)]
        down = [(j, i) for i, j in up]
        return lax.ppermute(last, axis, up), lax.ppermute(first, axis, down)

    left, right = beside(left_cols, right_cols, "col")
    last = right.shape[0] - RAD
    top, bottom = beside(
        jnp.concatenate([top_rows, right[:RAD], left[:RAD]], axis=1),
        jnp.concatenate([bottom_rows, right[last:], left[last:]], axis=1),
        "row",
    )
    r, c = lax.axis_index("row"), lax.axis_index("col")
    inside = jnp.stack([r > 0, r < lax.axis_size("row") - 1, c > 0, c < lax.axis_size("col") - 1])
    return top, bottom, left, right, jnp.broadcast_to(inside.astype(F32)[:, None], (4, 128))


def spread(x_ref, left, right, out_ref, rows, cols):
    for b in range(cols // BLK + 1):
        if b == 0:
            piece = jnp.concatenate([left, x_ref[:, 0:RAD]], axis=1)
        elif b == cols // BLK:
            piece = jnp.concatenate([x_ref[:, cols - RAD : cols], right], axis=1)
        else:
            piece = x_ref[:, BLK * b - RAD : BLK * b + RAD]
        out_ref[pl.ds(b, rows, stride=PITCH), :] = jnp.concatenate([piece] * 4, axis=1)
    for b in range(cols // BLK + 1, PITCH):
        out_ref[pl.ds(b, rows, stride=PITCH), :] = jnp.zeros((rows, 128), F32)


def windows(mask, s_ref, first, cols):
    count = mask.shape[0]
    lane = iota((count, 128), 1)
    tiles = [mask[:, 128 * q : 128 * q + 128] for q in range(cols // 128 + 1)]
    turned = [[x] + [pltpu.roll(x, 128 - BLK * j, 1) for j in (1, 2, 3)] for x in tiles]
    for b in range(cols // BLK + 1):
        if b == 0:
            low = jnp.where(lane < 32, turned[-1][1], turned[0][3])
            high = jnp.where(lane < 96, turned[-1][3], turned[0][1])
        else:
            q, j = divmod(b - 1, 4)
            x = turned[q]
            if j < 3:
                low, high = x[j], x[(j + 2) % 4]
            else:
                y = turned[q + 1]
                low = jnp.where(lane < 32, x[3], y[3])
                high = jnp.where(lane < 96, x[1], y[1])
        value = jnp.where(lane < 64, low, high)
        s_ref[pl.ds(first * PITCH + b, count, stride=PITCH), :] = value
    for b in range(cols // BLK + 1, PITCH):
        s_ref[pl.ds(first * PITCH + b, count, stride=PITCH), :] = jnp.zeros((count, 128), F32)


def group_rows(s_ref, a_ref, start, end, step):
    first_half = iota((step, 128), 1) < 64
    for m in range(start, end, step):
        for h in range(GROUP // 2):
            even = s_ref[m + 2 * h * PITCH : m + 2 * h * PITCH + step, :]
            odd = s_ref[m + (2 * h + 1) * PITCH : m + (2 * h + 1) * PITCH + step, :]
            a_ref[m : m + step, 128 * h : 128 * h + 128] = jnp.where(first_half, even, odd).astype(BF16)


def correlate(a_ref, starts, count, table_ref):
    fields = None
    for g in range(0, KS, GROUP):
        taken = min(GROUP, KS - g)
        right = table_ref[g : g + taken].reshape(taken * 2 * BLK, 256)
        if taken % 2:
            right = jnp.concatenate([right, jnp.zeros((2 * BLK, 256), BF16)], axis=0)
        lanes = slice(0, right.shape[0])
        parts = [a_ref[m + PITCH * g : m + PITCH * g + count, lanes] for m in starts]
        left = parts[0] if len(parts) == 1 else jnp.concatenate(parts, axis=0)
        term = jnp.dot(left, right, preferred_element_type=F32)
        fields = term if fields is None else fields + term
    return fields


def resist_and_gradient(fields, signed, wv, gs_ref, at):
    weighted = fields * wv
    square = fields * weighted
    intensity = square[:, :128] + square[:, 128:]
    intensity = intensity + pltpu.roll(intensity, 64, 1)
    intensity = intensity + pltpu.roll(intensity, 32, 1)
    resist = 1.0 / (1.0 + jnp.exp(3.0 - intensity))
    miss = resist - jnp.where(signed > 0.0, 1.0, 0.0)
    pull = jnp.abs(signed) * miss
    slope = 4.0 * pull * (resist * (1.0 - resist))
    for h in range(2):
        lanes = slice(128 * h, 128 * h + 128)
        gs_ref[at : at + fields.shape[0], lanes] = (weighted[:, lanes] * slope).astype(gs_ref.dtype)
    return miss, pull


def imaging_kernel(
    inbox_ref, table_ref, signed_ref, left_ref, right_ref, inside_ref, wv_ref,
    loss_ref, edges_ref, gs_ref, mask_ref, s_ref, a_ref, sw_ref,
):
    rows, cols = signed_ref.shape
    halo = 2 * RAD
    tall = rows + 2 * halo
    words = [inbox_ref[:, 0, :].T, inbox_ref[:, 1, :].T]
    lower = [(x & 0xFFFF).astype(F32) * 0.25 for x in words]
    upper = [(x >> 16).astype(F32) * 0.25 for x in words]
    cell = iota((BLK, 128), 0).astype(F32).astype(BF16)
    cell_end = (iota((BLK, 128), 0) + 1).astype(F32).astype(BF16)

    def covers(group, at, first, count):
        low8, high8 = lower[group][at : at + CAP, :], upper[group][at : at + CAP, :]
        stacked = []
        for base in range(first, first + count, BLK):
            low = jnp.clip(low8 - float(base), 0.0, float(BLK))
            high = jnp.clip(high8 - float(base), 0.0, float(BLK))
            parts = []
            for rank in range(CAP):
                lo = jnp.broadcast_to(low[rank : rank + 1, :], (BLK, 128)).astype(BF16)
                hi = jnp.broadcast_to(high[rank : rank + 1, :], (BLK, 128)).astype(BF16)
                parts.append(jnp.maximum(jnp.minimum(hi, cell_end) - jnp.maximum(lo, cell), 0.0))
            stacked.append(jnp.concatenate(parts, axis=1))
        return stacked[0] if len(stacked) == 1 else jnp.concatenate(stacked, axis=0)

    row_span = {-1: (rows - halo, halo, 0), 0: (0, rows, halo), 1: (0, halo, halo + rows)}
    col_span = {-1: (cols - halo, halo, cols + halo), 0: (0, cols, 0), 1: (0, halo, cols)}
    for n, (dr, dc) in enumerate(NEIGHBOURS + [(0, 0)]):
        group, at = (1, 0) if n == 8 else (0, 16 * n)
        r_first, r_count, r_at = row_span[dr]
        c_first, c_count, c_at = col_span[dc]
        row_cover = covers(group, at + 8, r_first, r_count)
        col_cover = covers(group, at, c_first, c_count)
        part = dot_nt(row_cover, col_cover).astype(BF16).astype(F32)
        mask_ref[r_at : r_at + r_count, c_at : c_at + c_count] = part

    edges_ref[0:64, :] = mask_ref[0:64, :].astype(BF16)
    edges_ref[64:112, :] = mask_ref[tall - 48 : tall, :].astype(BF16)
    windows(mask_ref[RAD : tall - RAD + 8, :], s_ref, RAD, cols)
    group_rows(s_ref, a_ref, RAD * PITCH, (tall - RAD) * PITCH, 16 * PITCH)
    left = jnp.where(inside_ref[2:3, 0:1] > 0.0, left_ref[...], 0.0)
    right = jnp.where(inside_ref[3:4, 0:1] > 0.0, right_ref[...], 0.0)
    spread(signed_ref, left, right, sw_ref, rows, cols)

    wv = wv_ref[...]
    chunk = rows // 8 * PITCH
    block = iota((chunk, 128), 0) % PITCH
    co = iota((chunk, 128), 1) & (BLK - 1)
    own = ((block > 0) | (co >= RAD)) & ((block < cols // BLK) | (co < RAD)) & (block <= cols // BLK)
    total = jnp.zeros((1, 128), F32)
    ahead = correlate(a_ref, [RAD * PITCH], chunk, table_ref)
    for k in range(8):
        m = k * chunk
        fields = ahead
        if k < 7:
            ahead = correlate(a_ref, [RAD * PITCH + m + chunk], chunk, table_ref)
        signed = sw_ref[m : m + chunk, :]
        miss, pull = resist_and_gradient(fields, signed, wv, gs_ref, m)
        part = jnp.where(own, pull * miss, 0.0)
        total = total + jnp.sum(part, axis=0, keepdims=True)
    total = 0.25 * jnp.sum(total, axis=1, keepdims=True)
    loss_ref[...] = jnp.broadcast_to(total, loss_ref.shape)


def imaging(inbox, table, signed, left, right, inside, wv, devices):
    rows, cols = signed.shape
    tall = rows + 4 * RAD
    return pl.pallas_call(
        imaging_kernel,
        out_shape=(
            pltpu.VMEM((devices, 1, 128), F32),
            pltpu.VMEM((112, cols + 128), BF16),
            pltpu.VMEM((rows * PITCH, 256), BF16),
        ),
        in_specs=[WHOLE] * 7,
        scratch_shapes=[
            pltpu.VMEM((tall, cols + 128), F32),
            pltpu.VMEM(((tall + 8) * PITCH, 128), F32),
            pltpu.VMEM((tall * PITCH, 64 * GROUP), BF16),
            pltpu.VMEM((rows * PITCH, 128), F32),
        ],
        compiler_params=pltpu.CompilerParams(vmem_limit_bytes=VMEM_LIMIT),
        cost_estimate=pl.CostEstimate(flops=4 * 10**9, bytes_accessed=8 * 10**6, transcendentals=10**6),
    )(inbox, table, signed, left, right, inside, wv)


def adjoint_taps(table_ref, start, at):
    first, last = max(start, 0), min(start + 8, KS)
    pieces = [table_ref[first:last, at : at + BLK, :].reshape((last - first) * BLK, 256)]
    if first > start:
        pieces.insert(0, jnp.zeros(((first - start) * BLK, 256), BF16))
    if last < start + 8:
        pieces.append(jnp.zeros(((start + 8 - last) * BLK, 256), BF16))
    return pieces[0] if len(pieces) == 1 else jnp.concatenate(pieces, axis=0)


def adjoint_kernel(
    edges_ref, table_ref, gs_ref, top_ref, bottom_ref, inside_ref, wv_ref,
    out_ref, s_ref, a_ref, x_ref, sw_ref, gw_ref, g_ref, acc_ref, tile_ref,
):
    rows, cols = out_ref.shape
    ext = rows + 2 * RAD
    x_ref[0:RAD, :] = jnp.where(inside_ref[0:1, 0:1] > 0.0, top_ref[...], 0.0)
    x_ref[RAD : 2 * RAD, :] = jnp.where(inside_ref[1:2, 0:1] > 0.0, bottom_ref[...], 0.0)
    left = jnp.where(inside_ref[2:3, 0:1] > 0.0, x_ref[:, cols + RAD : cols + 2 * RAD], 0.0)
    right = jnp.where(inside_ref[3:4, 0:1] > 0.0, x_ref[:, cols : cols + RAD], 0.0)
    spread(x_ref, left, right, sw_ref, 2 * RAD, cols)
    s_ref[112 * PITCH :, :] = jnp.zeros((8 * PITCH, 128), F32)
    windows(edges_ref[0:64, :].astype(F32), s_ref, 0, cols)
    windows(edges_ref[64:112, :].astype(F32), s_ref, 64, cols)
    group_rows(s_ref, a_ref, 0, 48 * PITCH, 16 * PITCH)
    group_rows(s_ref, a_ref, 64 * PITCH, 112 * PITCH, 16 * PITCH)
    fields = correlate(a_ref, [0, 64 * PITCH], RAD * PITCH, table_ref)
    resist_and_gradient(fields, sw_ref[...], wv_ref[...], gw_ref, 0)
    gw_ref[2 * RAD * PITCH :, :] = gs_ref[...].astype(F32)

    for r in range(ext):
        for s in range(2):
            if r < RAD:
                row = r
            elif r >= RAD + rows:
                row = r - rows
            else:
                row = r + RAD
            at = row * PITCH + s
            g_ref[s, r % 8, r // 8] = gw_ref[at : at + 16, :].astype(BF16)

    total = jnp.zeros((256, 256), F32)
    for i in range(40):
        for s in range(2):
            fields = g_ref[s, i % 8, i // 8 : i // 8 + 16].reshape(256, 256)
            total = total + dot_nt(fields, adjoint_taps(table_ref, KS - 1 - i, BLK * (1 - s)))
    for h in range(2):
        acc_ref[h] = total[:, 128 * h : 128 * h + 128]
    for q in range(cols // 128):
        for h in range(2):
            per_block = [acc_ref[h, pl.ds(4 * q + j, 16, stride=16), :] for j in range(4)]
            for j in range(4):
                pieces = [x[:, BLK * j : BLK * j + BLK] for x in per_block]
                tile_ref[q, pl.ds(4 * h + j, 16, stride=8), :] = jnp.concatenate(pieces, axis=1)
        out_ref[:, 128 * q : 128 * q + 128] = tile_ref[q]


def adjoint(edges, table, gs, top, bottom, inside, wv, rows, cols):
    ext = rows + 2 * RAD
    return pl.pallas_call(
        adjoint_kernel,
        out_shape=jax.ShapeDtypeStruct((rows, cols), F32),
        in_specs=[WHOLE] * 7,
        scratch_shapes=[
            pltpu.VMEM((120 * PITCH, 128), F32),
            pltpu.VMEM((112 * PITCH, 64 * GROUP), BF16),
            pltpu.VMEM((2 * RAD, cols + 2 * RAD), F32),
            pltpu.VMEM((2 * RAD * PITCH, 128), F32),
            pltpu.VMEM((ext * PITCH, 256), F32),
            pltpu.VMEM((2, 8, ext // 8, 16, 256), BF16),
            pltpu.VMEM((2, 256, 128), F32),
            pltpu.VMEM((cols // 128, rows, 128), F32),
        ],
        compiler_params=pltpu.CompilerParams(vmem_limit_bytes=VMEM_LIMIT),
        cost_estimate=pl.CostEstimate(flops=4 * 10**9, bytes_accessed=10**7, transcendentals=0),
    )(edges, table, gs, top, bottom, inside, wv)


def shards(rects, owner, counts, target, loss_weight, kernel, socs_weight):
    row_devices = lax.axis_size("row")
    col_devices = lax.axis_size("col")
    devices = row_devices * col_devices
    rows, cols = target.shape
    outbox, signed, *strips = make_outbox(rects, owner, counts, target, loss_weight, devices, col_devices)
    inbox = lax.all_to_all(outbox, ("row", "col"), split_axis=0, concat_axis=0, tiled=True)
    table = make_tables(kernel)
    top, bottom, left, right, inside = weight_strips(*strips)
    wv = jnp.repeat(socs_weight, 2 * BLK).reshape(1, kernel.shape[0] * BLK)
    local, edges, gs = imaging(inbox, table, signed, left, right, inside, wv, devices)
    losses = lax.all_to_all(local, ("row", "col"), split_axis=0, concat_axis=0, tiled=True)
    mask_grad = adjoint(edges, table, gs, top, bottom, inside, wv, rows, cols)
    window_area = rows * row_devices * cols * col_devices
    return (mask_grad, (jnp.sum(losses[:, 0, 0]) / window_area).reshape(1))


def solution(mesh):
    placed = (
        P(None, ("row", "col")),
        P(("row", "col")),
        P(("row", "col")),
        P("row", "col"),
        P("row", "col"),
        P(),
        P(),
    )
    return jax.shard_map(
        shards, mesh=mesh, in_specs=placed, out_specs=(P("row", "col"), P()), check_vma=False
    )
```

```python
import jax
import jax.numpy as jnp
from jax import lax
from jax.experimental import pallas as pl
from jax.experimental.pallas import tpu as pltpu
from jax.sharding import PartitionSpec as P

RAD = 16
CAP = 8
KS = 33
BLK = 32
GROUP = 8
WIDE = 2 * BLK + 1
PITCH = 18
NEIGHBOURS = [(dr, dc) for dr in (-1, 0, 1) for dc in (-1, 0, 1) if (dr, dc) != (0, 0)]
F32 = jnp.float32
BF16 = jnp.bfloat16
VMEM_LIMIT = 32 * 1024 * 1024


def dot_nt(a, b):
    return lax.dot_general(a, b, (((1,), (1,)), ((), ())), preferred_element_type=F32)


def iota(shape, dim):
    return lax.broadcasted_iota(jnp.int32, shape, dim)


def outbox_kernel(
    tile_cols, counts_ref, rects_ref, owner_ref, target_ref, weight_ref,
    out_ref, signed_ref, top_ref, bottom_ref, left_ref, right_ref,
    pad_ref, box_ref, target_buf, weight_buf, sems,
):
    rows, cols = signed_ref.shape
    load_target = pltpu.make_async_copy(target_ref, target_buf, sems.at[0])
    load_weight = pltpu.make_async_copy(weight_ref, weight_buf, sems.at[1])
    load_target.start()
    load_weight.start()
    slots = owner_ref.shape[1]
    tiles = out_ref.shape[0]
    live = iota((1, slots), 1) < counts_ref[0]
    own = jnp.where(live, owner_ref[...], -1)
    hit = iota((tiles, slots), 0) == own
    hits = jnp.where(hit, 1.0, 0.0).astype(BF16)
    before = jnp.where(iota((slots, slots), 0) < iota((slots, slots), 1), 1.0, 0.0).astype(BF16)
    earlier = jnp.dot(hits, before, preferred_element_type=F32)
    rank = jnp.sum(jnp.where(hit, earlier, 0.0), axis=0, keepdims=True).astype(jnp.int32)
    row = iota((16, slots), 0)
    chosen = rank == (row & 7)
    vertical = (row & 8) == 8

    def placed(first, second):
        value = jnp.where(vertical, second, first)
        value = jnp.where(chosen, value, 0)
        high = (value >> 4).astype(F32).astype(BF16)
        low = (value & 15).astype(F32).astype(BF16)
        return (16.0 * dot_nt(hits, high) + dot_nt(hits, low)).astype(jnp.int32)

    lower = placed(rects_ref[0:1, :], rects_ref[2:3, :])
    upper = placed(rects_ref[1:2, :], rects_ref[3:4, :])
    word = lower + (upper << 16)
    word = jnp.concatenate([word] * 8, axis=1)
    pad_ref[...] = jnp.zeros(pad_ref.shape, jnp.int32)
    pad_ref[24 : 24 + tiles, :] = word
    column = iota((tiles, 128), 0) % tile_cols
    group = iota((tiles, 128), 1) >> 4
    result = jnp.zeros((tiles, 128), jnp.int32)
    for n, (dr, dc) in enumerate(NEIGHBOURS):
        start = 24 + dr * tile_cols + dc
        inside = (column + dc >= 0) & (column + dc < tile_cols) & (group == n)
        result = jnp.where(inside, pad_ref[start : start + tiles, :], result)
    box_ref[:, 0, :] = result
    box_ref[:, 1, :] = word
    store = pltpu.make_async_copy(box_ref, out_ref, sems.at[2])
    store.start()
    load_target.wait()
    load_weight.wait()
    signed_ref[...] = jnp.where(target_buf[...] > 0, weight_buf[...], -weight_buf[...])
    top_ref[...] = signed_ref[0:RAD, :]
    bottom_ref[...] = signed_ref[rows - RAD : rows, :]
    left_ref[...] = signed_ref[:, 0:RAD]
    right_ref[...] = signed_ref[:, cols - RAD : cols]
    store.wait()


SMALL = pl.BlockSpec(memory_space=pltpu.SMEM)
WHOLE = pl.BlockSpec(memory_space=pltpu.VMEM)
ANYWHERE = pl.BlockSpec(memory_space=pl.ANY)


def make_outbox(rects, owner, counts, target, weight, tiles, tile_cols):
    slots = owner.shape[0]
    rows, cols = target.shape
    return pl.pallas_call(
        lambda *refs: outbox_kernel(tile_cols, *refs),
        out_shape=(
            jax.ShapeDtypeStruct((tiles, 2, 128), jnp.int32),
            pltpu.VMEM((rows, cols), F32),
            pltpu.VMEM((RAD, cols), F32),
            pltpu.VMEM((RAD, cols), F32),
            pltpu.VMEM((rows, RAD), F32),
            pltpu.VMEM((rows, RAD), F32),
        ),
        in_specs=[SMALL, WHOLE, WHOLE, ANYWHERE, ANYWHERE],
        out_specs=(ANYWHERE,) + (WHOLE,) * 5,
        scratch_shapes=[
            pltpu.VMEM((tiles + 48, 128), jnp.int32),
            pltpu.VMEM((tiles, 2, 128), jnp.int32),
            pltpu.VMEM((rows, cols), jnp.int32),
            pltpu.VMEM((rows, cols), F32),
            pltpu.SemaphoreType.DMA((3,)),
        ],
        cost_estimate=pl.CostEstimate(flops=10**8, bytes_accessed=10**6, transcendentals=0),
    )(counts, rects, owner.reshape(1, slots), target, weight)


def tables_kernel(kernel_ref, table_ref, wide_ref):
    channels = kernel_ref.shape[1]
    lanes = channels * BLK
    tap, lane = iota((KS, lanes), 0), iota((KS, lanes), 1) % BLK
    flat = kernel_ref[...].astype(F32).reshape(KS * channels, KS).astype(BF16)
    mine = iota((KS, channels, lanes), 1) == iota((KS, channels, lanes), 2) // BLK

    def by_lane(picked):
        every = jnp.dot(flat, jnp.where(picked, 1.0, 0.0).astype(BF16), preferred_element_type=F32)
        return jnp.sum(jnp.where(mine, every.reshape(KS, channels, lanes), 0.0), axis=1)

    taps = by_lane(tap == KS - 1 - lane)
    edge = by_lane(tap == 0)
    co = iota((KS, 128), 1) % BLK
    for p in range(BLK):
        for h in range(lanes // 128):
            mine = taps[:, 128 * h : 128 * h + 128]
            ends = edge[:, 128 * h : 128 * h + 128]
            near = pltpu.roll(mine, p, 1) if p else mine
            far = pltpu.roll(mine, p + 128 - BLK, 1)
            far = jnp.where(co < p, far, jnp.where(co == p, ends, 0.0))
            wide_ref[h, pl.ds(p, KS, stride=WIDE), :] = far
            wide_ref[h, pl.ds(BLK + p, KS, stride=WIDE), :] = jnp.where(co >= p, near, 0.0)
    for a in range(KS):
        for h in range(lanes // 128):
            table_ref[a, :, 128 * h : 128 * h + 128] = wide_ref[h, a * WIDE : a * WIDE + 2 * BLK, :].astype(BF16)


def make_tables(kernel):
    lanes = kernel.shape[0] * BLK
    return pl.pallas_call(
        tables_kernel,
        out_shape=pltpu.VMEM((KS, 2 * BLK, lanes), BF16),
        in_specs=[WHOLE],
        scratch_shapes=[pltpu.VMEM((lanes // 128, KS * WIDE + 8, 128), F32)],
        compiler_params=pltpu.CompilerParams(vmem_limit_bytes=VMEM_LIMIT // 2),
        cost_estimate=pl.CostEstimate(flops=10**10, bytes_accessed=10**6, transcendentals=0),
    )(kernel.transpose(1, 0, 2))


def weight_strips(top_rows, bottom_rows, left_cols, right_cols):
    def beside(first, last, axis):
        count = lax.axis_size(axis)
        up = [(i, (i + 1) % count) for i in range(count)]
        down = [(j, i) for i, j in up]
        return lax.ppermute(last, axis, up), lax.ppermute(first, axis, down)

    left, right = beside(left_cols, right_cols, "col")
    last = right.shape[0] - RAD
    top, bottom = beside(
        jnp.concatenate([top_rows, right[:RAD], left[:RAD]], axis=1),
        jnp.concatenate([bottom_rows, right[last:], left[last:]], axis=1),
        "row",
    )
    r, c = lax.axis_index("row"), lax.axis_index("col")
    inside = jnp.stack([r > 0, r < lax.axis_size("row") - 1, c > 0, c < lax.axis_size("col") - 1])
    return top, bottom, left, right, jnp.broadcast_to(inside.astype(F32)[:, None], (4, 128))


def spread(x_ref, left, right, out_ref, rows, cols):
    for b in range(cols // BLK + 1):
        if b == 0:
            piece = jnp.concatenate([left, x_ref[:, 0:RAD]], axis=1)
        elif b == cols // BLK:
            piece = jnp.concatenate([x_ref[:, cols - RAD : cols], right], axis=1)
        else:
            piece = x_ref[:, BLK * b - RAD : BLK * b + RAD]
        out_ref[pl.ds(b, rows, stride=PITCH), :] = jnp.concatenate([piece] * 4, axis=1)
    for b in range(cols // BLK + 1, PITCH):
        out_ref[pl.ds(b, rows, stride=PITCH), :] = jnp.zeros((rows, 128), F32)


def windows(mask, s_ref, first, cols):
    count = mask.shape[0]
    lane = iota((count, 128), 1)
    tiles = [mask[:, 128 * q : 128 * q + 128] for q in range(cols // 128 + 1)]
    turned = [[x] + [pltpu.roll(x, 128 - BLK * j, 1) for j in (1, 2, 3)] for x in tiles]
    for b in range(cols // BLK + 1):
        if b == 0:
            low = jnp.where(lane < 32, turned[-1][1], turned[0][3])
            high = jnp.where(lane < 96, turned[-1][3], turned[0][1])
        else:
            q, j = divmod(b - 1, 4)
            x = turned[q]
            if j < 3:
                low, high = x[j], x[(j + 2) % 4]
            else:
                y = turned[q + 1]
                low = jnp.where(lane < 32, x[3], y[3])
                high = jnp.where(lane < 96, x[1], y[1])
        value = jnp.where(lane < 64, low, high)
        s_ref[pl.ds(first * PITCH + b, count, stride=PITCH), :] = value
    for b in range(cols // BLK + 1, PITCH):
        s_ref[pl.ds(first * PITCH + b, count, stride=PITCH), :] = jnp.zeros((count, 128), F32)


def group_rows(s_ref, a_ref, start, end, step):
    first_half = iota((step, 128), 1) < 64
    for m in range(start, end, step):
        for h in range(GROUP // 2):
            even = s_ref[m + 2 * h * PITCH : m + 2 * h * PITCH + step, :]
            odd = s_ref[m + (2 * h + 1) * PITCH : m + (2 * h + 1) * PITCH + step, :]
            a_ref[m : m + step, 128 * h : 128 * h + 128] = jnp.where(first_half, even, odd).astype(BF16)


def correlate(a_ref, starts, count, table_ref):
    fields = None
    for g in range(0, KS, GROUP):
        taken = min(GROUP, KS - g)
        right = table_ref[g : g + taken].reshape(taken * 2 * BLK, 256)
        if taken % 2:
            right = jnp.concatenate([right, jnp.zeros((2 * BLK, 256), BF16)], axis=0)
        lanes = slice(0, right.shape[0])
        parts = [a_ref[m + PITCH * g : m + PITCH * g + count, lanes] for m in starts]
        left = parts[0] if len(parts) == 1 else jnp.concatenate(parts, axis=0)
        term = jnp.dot(left, right, preferred_element_type=F32)
        fields = term if fields is None else fields + term
    return fields


def resist_and_gradient(fields, signed, wv, gs_ref, at):
    weighted = fields * wv
    square = fields * weighted
    intensity = square[:, :128] + square[:, 128:]
    intensity = intensity + pltpu.roll(intensity, 64, 1)
    intensity = intensity + pltpu.roll(intensity, 32, 1)
    resist = 1.0 / (1.0 + jnp.exp(3.0 - intensity))
    miss = resist - jnp.where(signed > 0.0, 1.0, 0.0)
    pull = jnp.abs(signed) * miss
    slope = 4.0 * pull * (resist * (1.0 - resist))
    for h in range(2):
        lanes = slice(128 * h, 128 * h + 128)
        gs_ref[at : at + fields.shape[0], lanes] = (weighted[:, lanes] * slope).astype(gs_ref.dtype)
    return miss, pull


def imaging_kernel(
    inbox_ref, table_ref, signed_ref, left_ref, right_ref, inside_ref, wv_ref,
    loss_ref, edges_ref, gs_ref, mask_ref, s_ref, a_ref, sw_ref,
):
    rows, cols = signed_ref.shape
    halo = 2 * RAD
    tall = rows + 2 * halo
    words = [inbox_ref[:, 0, :].T, inbox_ref[:, 1, :].T]
    lower = [(x & 0xFFFF).astype(F32) * 0.25 for x in words]
    upper = [(x >> 16).astype(F32) * 0.25 for x in words]
    cell = iota((BLK, 128), 0).astype(F32).astype(BF16)
    cell_end = (iota((BLK, 128), 0) + 1).astype(F32).astype(BF16)

    def covers(group, at, first, count):
        low8, high8 = lower[group][at : at + CAP, :], upper[group][at : at + CAP, :]
        stacked = []
        for base in range(first, first + count, BLK):
            low = jnp.clip(low8 - float(base), 0.0, float(BLK))
            high = jnp.clip(high8 - float(base), 0.0, float(BLK))
            parts = []
            for rank in range(CAP):
                lo = jnp.broadcast_to(low[rank : rank + 1, :], (BLK, 128)).astype(BF16)
                hi = jnp.broadcast_to(high[rank : rank + 1, :], (BLK, 128)).astype(BF16)
                parts.append(jnp.maximum(jnp.minimum(hi, cell_end) - jnp.maximum(lo, cell), 0.0))
            stacked.append(jnp.concatenate(parts, axis=1))
        return stacked[0] if len(stacked) == 1 else jnp.concatenate(stacked, axis=0)

    row_span = {-1: (rows - halo, halo, 0), 0: (0, rows, halo), 1: (0, halo, halo + rows)}
    col_span = {-1: (cols - halo, halo, cols + halo), 0: (0, cols, 0), 1: (0, halo, cols)}
    for n, (dr, dc) in enumerate(NEIGHBOURS + [(0, 0)]):
        group, at = (1, 0) if n == 8 else (0, 16 * n)
        r_first, r_count, r_at = row_span[dr]
        c_first, c_count, c_at = col_span[dc]
        row_cover = covers(group, at + 8, r_first, r_count)
        col_cover = covers(group, at, c_first, c_count)
        part = dot_nt(row_cover, col_cover).astype(BF16).astype(F32)
        mask_ref[r_at : r_at + r_count, c_at : c_at + c_count] = part

    edges_ref[0:64, :] = mask_ref[0:64, :].astype(BF16)
    edges_ref[64:112, :] = mask_ref[tall - 48 : tall, :].astype(BF16)
    windows(mask_ref[RAD : tall - RAD + 8, :], s_ref, RAD, cols)
    group_rows(s_ref, a_ref, RAD * PITCH, (tall - RAD) * PITCH, 16 * PITCH)
    left = jnp.where(inside_ref[2:3, 0:1] > 0.0, left_ref[...], 0.0)
    right = jnp.where(inside_ref[3:4, 0:1] > 0.0, right_ref[...], 0.0)
    spread(signed_ref, left, right, sw_ref, rows, cols)

    wv = wv_ref[...]
    chunk = rows // 8 * PITCH
    block = iota((chunk, 128), 0) % PITCH
    co = iota((chunk, 128), 1) & (BLK - 1)
    own = ((block > 0) | (co >= RAD)) & ((block < cols // BLK) | (co < RAD)) & (block <= cols // BLK)
    total = jnp.zeros((1, 128), F32)
    ahead = correlate(a_ref, [RAD * PITCH], chunk, table_ref)
    for k in range(8):
        m = k * chunk
        fields = ahead
        if k < 7:
            ahead = correlate(a_ref, [RAD * PITCH + m + chunk], chunk, table_ref)
        signed = sw_ref[m : m + chunk, :]
        miss, pull = resist_and_gradient(fields, signed, wv, gs_ref, m)
        part = jnp.where(own, pull * miss, 0.0)
        total = total + jnp.sum(part, axis=0, keepdims=True)
    total = 0.25 * jnp.sum(total, axis=1, keepdims=True)
    loss_ref[...] = jnp.broadcast_to(total, loss_ref.shape)


def imaging(inbox, table, signed, left, right, inside, wv, devices):
    rows, cols = signed.shape
    tall = rows + 4 * RAD
    return pl.pallas_call(
        imaging_kernel,
        out_shape=(
            pltpu.VMEM((devices, 1, 128), F32),
            pltpu.VMEM((112, cols + 128), BF16),
            pltpu.VMEM((rows * PITCH, 256), BF16),
        ),
        in_specs=[WHOLE] * 7,
        scratch_shapes=[
            pltpu.VMEM((tall, cols + 128), F32),
            pltpu.VMEM(((tall + 8) * PITCH, 128), F32),
            pltpu.VMEM((tall * PITCH, 64 * GROUP), BF16),
            pltpu.VMEM((rows * PITCH, 128), F32),
        ],
        compiler_params=pltpu.CompilerParams(vmem_limit_bytes=VMEM_LIMIT),
        cost_estimate=pl.CostEstimate(flops=4 * 10**9, bytes_accessed=8 * 10**6, transcendentals=10**6),
    )(inbox, table, signed, left, right, inside, wv)


def adjoint_taps(table_ref, start, at):
    first, last = max(start, 0), min(start + 8, KS)
    pieces = [table_ref[first:last, at : at + BLK, :].reshape((last - first) * BLK, 256)]
    if first > start:
        pieces.insert(0, jnp.zeros(((first - start) * BLK, 256), BF16))
    if last < start + 8:
        pieces.append(jnp.zeros(((start + 8 - last) * BLK, 256), BF16))
    return pieces[0] if len(pieces) == 1 else jnp.concatenate(pieces, axis=0)


def adjoint_kernel(
    edges_ref, table_ref, gs_ref, top_ref, bottom_ref, inside_ref, wv_ref,
    out_ref, s_ref, a_ref, x_ref, sw_ref, gw_ref, g_ref, acc_ref, tile_ref,
):
    rows, cols = out_ref.shape
    ext = rows + 2 * RAD
    x_ref[0:RAD, :] = jnp.where(inside_ref[0:1, 0:1] > 0.0, top_ref[...], 0.0)
    x_ref[RAD : 2 * RAD, :] = jnp.where(inside_ref[1:2, 0:1] > 0.0, bottom_ref[...], 0.0)
    left = jnp.where(inside_ref[2:3, 0:1] > 0.0, x_ref[:, cols + RAD : cols + 2 * RAD], 0.0)
    right = jnp.where(inside_ref[3:4, 0:1] > 0.0, x_ref[:, cols : cols + RAD], 0.0)
    spread(x_ref, left, right, sw_ref, 2 * RAD, cols)
    s_ref[112 * PITCH :, :] = jnp.zeros((8 * PITCH, 128), F32)
    windows(edges_ref[0:64, :].astype(F32), s_ref, 0, cols)
    windows(edges_ref[64:112, :].astype(F32), s_ref, 64, cols)
    group_rows(s_ref, a_ref, 0, 48 * PITCH, 16 * PITCH)
    group_rows(s_ref, a_ref, 64 * PITCH, 112 * PITCH, 16 * PITCH)
    fields = correlate(a_ref, [0, 64 * PITCH], RAD * PITCH, table_ref)
    resist_and_gradient(fields, sw_ref[...], wv_ref[...], gw_ref, 0)
    gw_ref[2 * RAD * PITCH :, :] = gs_ref[...].astype(F32)

    for r in range(ext):
        for s in range(2):
            if r < RAD:
                row = r
            elif r >= RAD + rows:
                row = r - rows
            else:
                row = r + RAD
            at = row * PITCH + s
            g_ref[s, r % 8, r // 8] = gw_ref[at : at + 16, :].astype(BF16)

    total = jnp.zeros((256, 256), F32)
    for i in range(40):
        for s in range(2):
            fields = g_ref[s, i % 8, i // 8 : i // 8 + 16].reshape(256, 256)
            total = total + dot_nt(fields, adjoint_taps(table_ref, KS - 1 - i, BLK * (1 - s)))
    for h in range(2):
        acc_ref[h] = total[:, 128 * h : 128 * h + 128]
    for q in range(cols // 128):
        for h in range(2):
            per_block = [acc_ref[h, pl.ds(4 * q + j, 16, stride=16), :] for j in range(4)]
            for j in range(4):
                pieces = [x[:, BLK * j : BLK * j + BLK] for x in per_block]
                tile_ref[q, pl.ds(4 * h + j, 16, stride=8), :] = jnp.concatenate(pieces, axis=1)
        out_ref[:, 128 * q : 128 * q + 128] = tile_ref[q]


def adjoint(edges, table, gs, top, bottom, inside, wv, rows, cols):
    ext = rows + 2 * RAD
    return pl.pallas_call(
        adjoint_kernel,
        out_shape=jax.ShapeDtypeStruct((rows, cols), F32),
        in_specs=[WHOLE] * 7,
        scratch_shapes=[
            pltpu.VMEM((120 * PITCH, 128), F32),
            pltpu.VMEM((112 * PITCH, 64 * GROUP), BF16),
            pltpu.VMEM((2 * RAD, cols + 2 * RAD), F32),
            pltpu.VMEM((2 * RAD * PITCH, 128), F32),
            pltpu.VMEM((ext * PITCH, 256), F32),
            pltpu.VMEM((2, 8, ext // 8, 16, 256), BF16),
            pltpu.VMEM((2, 256, 128), F32),
            pltpu.VMEM((cols // 128, rows, 128), F32),
        ],
        compiler_params=pltpu.CompilerParams(vmem_limit_bytes=VMEM_LIMIT),
        cost_estimate=pl.CostEstimate(flops=4 * 10**9, bytes_accessed=10**7, transcendentals=0),
    )(edges, table, gs, top, bottom, inside, wv)


def shards(rects, owner, counts, target, loss_weight, kernel, socs_weight):
    row_devices = lax.axis_size("row")
    col_devices = lax.axis_size("col")
    devices = row_devices * col_devices
    rows, cols = target.shape
    outbox, signed, *strips = make_outbox(rects, owner, counts, target, loss_weight, devices, col_devices)
    inbox = lax.all_to_all(outbox, ("row", "col"), split_axis=0, concat_axis=0, tiled=True)
    table = make_tables(kernel)
    top, bottom, left, right, inside = weight_strips(*strips)
    wv = jnp.repeat(socs_weight, 2 * BLK).reshape(1, kernel.shape[0] * BLK)
    local, edges, gs = imaging(inbox, table, signed, left, right, inside, wv, devices)
    losses = lax.all_to_all(local, ("row", "col"), split_axis=0, concat_axis=0, tiled=True)
    mask_grad = adjoint(edges, table, gs, top, bottom, inside, wv, rows, cols)
    window_area = rows * row_devices * cols * col_devices
    return (mask_grad, (jnp.sum(losses[:, 0, 0]) / window_area).reshape(1))


def solution(mesh):
    placed = (
        P(None, ("row", "col")),
        P(("row", "col")),
        P(("row", "col")),
        P("row", "col"),
        P("row", "col"),
        P(),
        P(),
    )
    return jax.shard_map(
        shards, mesh=mesh, in_specs=placed, out_specs=(P("row", "col"), P()), check_vma=False
    )
```

```python
import jax
import jax.numpy as jnp
from jax import lax
from jax.experimental import pallas as pl
from jax.experimental.pallas import tpu as pltpu
from jax.sharding import PartitionSpec as P

RAD = 16
CAP = 8
KS = 33
BLK = 32
GROUP = 8
WIDE = 2 * BLK + 1
PITCH = 18
NEIGHBOURS = [(dr, dc) for dr in (-1, 0, 1) for dc in (-1, 0, 1) if (dr, dc) != (0, 0)]
F32 = jnp.float32
BF16 = jnp.bfloat16
VMEM_LIMIT = 32 * 1024 * 1024


def dot_nt(a, b):
    return lax.dot_general(a, b, (((1,), (1,)), ((), ())), preferred_element_type=F32)


def iota(shape, dim):
    return lax.broadcasted_iota(jnp.int32, shape, dim)


def outbox_kernel(
    tile_cols, counts_ref, rects_ref, owner_ref, target_ref, weight_ref, kernel_ref,
    out_ref, signed_ref, top_ref, bottom_ref, left_ref, right_ref, kernel_out_ref,
    pad_ref, box_ref, target_buf, weight_buf, sems,
):
    rows, cols = signed_ref.shape
    load_target = pltpu.make_async_copy(target_ref, target_buf, sems.at[0])
    load_weight = pltpu.make_async_copy(weight_ref, weight_buf, sems.at[1])
    load_target.start()
    load_weight.start()
    load_kernel = pltpu.make_async_copy(kernel_ref, kernel_out_ref, sems.at[3])
    load_kernel.start()
    slots = owner_ref.shape[1]
    tiles = out_ref.shape[0]
    live = iota((1, slots), 1) < counts_ref[0]
    own = jnp.where(live, owner_ref[...], -1)
    hit = iota((tiles, slots), 0) == own
    hits = jnp.where(hit, 1.0, 0.0).astype(BF16)
    before = jnp.where(iota((slots, slots), 0) < iota((slots, slots), 1), 1.0, 0.0).astype(BF16)
    earlier = jnp.dot(hits, before, preferred_element_type=F32)
    rank = jnp.sum(jnp.where(hit, earlier, 0.0), axis=0, keepdims=True).astype(jnp.int32)
    row = iota((16, slots), 0)
    chosen = rank == (row & 7)
    vertical = (row & 8) == 8

    def placed(first, second):
        value = jnp.where(vertical, second, first)
        value = jnp.where(chosen, value, 0)
        high = (value >> 4).astype(F32).astype(BF16)
        low = (value & 15).astype(F32).astype(BF16)
        return (16.0 * dot_nt(hits, high) + dot_nt(hits, low)).astype(jnp.int32)

    lower = placed(rects_ref[0:1, :], rects_ref[2:3, :])
    upper = placed(rects_ref[1:2, :], rects_ref[3:4, :])
    word = lower + (upper << 16)
    word = jnp.concatenate([word] * 8, axis=1)
    pad_ref[...] = jnp.zeros(pad_ref.shape, jnp.int32)
    pad_ref[24 : 24 + tiles, :] = word
    column = iota((tiles, 128), 0) % tile_cols
    group = iota((tiles, 128), 1) >> 4
    result = jnp.zeros((tiles, 128), jnp.int32)
    for n, (dr, dc) in enumerate(NEIGHBOURS):
        start = 24 + dr * tile_cols + dc
        inside = (column + dc >= 0) & (column + dc < tile_cols) & (group == n)
        result = jnp.where(inside, pad_ref[start : start + tiles, :], result)
    box_ref[:, 0, :] = result
    box_ref[:, 1, :] = word
    store = pltpu.make_async_copy(box_ref, out_ref, sems.at[2])
    store.start()
    load_target.wait()
    load_weight.wait()
    signed_ref[...] = jnp.where(target_buf[...] > 0, weight_buf[...], -weight_buf[...])
    top_ref[...] = signed_ref[0:RAD, :]
    bottom_ref[...] = signed_ref[rows - RAD : rows, :]
    left_ref[...] = signed_ref[:, 0:RAD]
    right_ref[...] = signed_ref[:, cols - RAD : cols]
    load_kernel.wait()
    store.wait()


SMALL = pl.BlockSpec(memory_space=pltpu.SMEM)
WHOLE = pl.BlockSpec(memory_space=pltpu.VMEM)
ANYWHERE = pl.BlockSpec(memory_space=pl.ANY)


def make_outbox(rects, owner, counts, target, weight, kernel, tiles, tile_cols):
    slots = owner.shape[0]
    rows, cols = target.shape
    return pl.pallas_call(
        lambda *refs: outbox_kernel(tile_cols, *refs),
        out_shape=(
            jax.ShapeDtypeStruct((tiles, 2, 128), jnp.int32),
            pltpu.VMEM((rows, cols), F32),
            pltpu.VMEM((RAD, cols), F32),
            pltpu.VMEM((RAD, cols), F32),
            pltpu.VMEM((rows, RAD), F32),
            pltpu.VMEM((rows, RAD), F32),
            pltpu.VMEM(kernel.shape, BF16),
        ),
        in_specs=[SMALL, WHOLE, WHOLE, ANYWHERE, ANYWHERE, ANYWHERE],
        out_specs=(ANYWHERE,) + (WHOLE,) * 6,
        scratch_shapes=[
            pltpu.VMEM((tiles + 48, 128), jnp.int32),
            pltpu.VMEM((tiles, 2, 128), jnp.int32),
            pltpu.VMEM((rows, cols), jnp.int32),
            pltpu.VMEM((rows, cols), F32),
            pltpu.SemaphoreType.DMA((4,)),
        ],
        cost_estimate=pl.CostEstimate(flops=10**8, bytes_accessed=10**6, transcendentals=0),
    )(counts, rects, owner.reshape(1, slots), target, weight, kernel)


def tables_kernel(kernel_ref, table_ref, wide_ref):
    channels = kernel_ref.shape[1]
    lanes = channels * BLK
    tap, lane = iota((KS, lanes), 0), iota((KS, lanes), 1) % BLK
    flat = kernel_ref[...].astype(F32).reshape(KS * channels, KS).astype(BF16)
    mine = iota((KS, channels, lanes), 1) == iota((KS, channels, lanes), 2) // BLK

    def by_lane(picked):
        every = jnp.dot(flat, jnp.where(picked, 1.0, 0.0).astype(BF16), preferred_element_type=F32)
        return jnp.sum(jnp.where(mine, every.reshape(KS, channels, lanes), 0.0), axis=1)

    taps = by_lane(tap == KS - 1 - lane)
    edge = by_lane(tap == 0)
    co = iota((KS, 128), 1) % BLK
    for p in range(BLK):
        for h in range(lanes // 128):
            mine = taps[:, 128 * h : 128 * h + 128]
            ends = edge[:, 128 * h : 128 * h + 128]
            near = pltpu.roll(mine, p, 1) if p else mine
            far = pltpu.roll(mine, p + 128 - BLK, 1)
            far = jnp.where(co < p, far, jnp.where(co == p, ends, 0.0))
            wide_ref[h, pl.ds(p, KS, stride=WIDE), :] = far
            wide_ref[h, pl.ds(BLK + p, KS, stride=WIDE), :] = jnp.where(co >= p, near, 0.0)
    for a in range(KS):
        for h in range(lanes // 128):
            table_ref[a, :, 128 * h : 128 * h + 128] = wide_ref[h, a * WIDE : a * WIDE + 2 * BLK, :].astype(BF16)


def make_tables(kernel):
    lanes = kernel.shape[1] * BLK
    return pl.pallas_call(
        tables_kernel,
        out_shape=pltpu.VMEM((KS, 2 * BLK, lanes), BF16),
        in_specs=[WHOLE],
        scratch_shapes=[pltpu.VMEM((lanes // 128, KS * WIDE + 8, 128), F32)],
        compiler_params=pltpu.CompilerParams(vmem_limit_bytes=VMEM_LIMIT // 2),
        cost_estimate=pl.CostEstimate(flops=10**10, bytes_accessed=10**6, transcendentals=0),
    )(kernel)


def weight_strips(top_rows, bottom_rows, left_cols, right_cols):
    def beside(first, last, axis):
        count = lax.axis_size(axis)
        up = [(i, (i + 1) % count) for i in range(count)]
        down = [(j, i) for i, j in up]
        return lax.ppermute(last, axis, up), lax.ppermute(first, axis, down)

    c = lax.axis_index("col")
    left_cols = jnp.where(c > 0, left_cols, 0.0)
    right_cols = jnp.where(c < lax.axis_size("col") - 1, right_cols, 0.0)
    left, right = beside(left_cols, right_cols, "col")
    last = right.shape[0] - RAD
    top, bottom = beside(
        jnp.concatenate([top_rows, right[:RAD], left[:RAD]], axis=1),
        jnp.concatenate([bottom_rows, right[last:], left[last:]], axis=1),
        "row",
    )
    r, c = lax.axis_index("row"), lax.axis_index("col")
    inside = jnp.stack([r > 0, r < lax.axis_size("row") - 1, c > 0, c < lax.axis_size("col") - 1])
    return top, bottom, left, right, jnp.broadcast_to(inside.astype(F32)[:, None], (4, 128))


def spread(x_ref, left, right, out_ref, rows, cols):
    for b in range(cols // BLK + 1):
        if b == 0:
            piece = jnp.concatenate([left, x_ref[:, 0:RAD]], axis=1)
        elif b == cols // BLK:
            piece = jnp.concatenate([x_ref[:, cols - RAD : cols], right], axis=1)
        else:
            piece = x_ref[:, BLK * b - RAD : BLK * b + RAD]
        out_ref[pl.ds(b, rows, stride=PITCH), :] = jnp.concatenate([piece] * 4, axis=1)
    for b in range(cols // BLK + 1, PITCH):
        out_ref[pl.ds(b, rows, stride=PITCH), :] = jnp.zeros((rows, 128), F32)


def windows(mask, s_ref, first, cols):
    count = mask.shape[0]
    lane = iota((count, 128), 1)
    tiles = [mask[:, 128 * q : 128 * q + 128] for q in range(cols // 128 + 1)]
    turned = [[x] + [pltpu.roll(x, 128 - BLK * j, 1) for j in (1, 2, 3)] for x in tiles]
    for b in range(cols // BLK + 1):
        if b == 0:
            low = jnp.where(lane < 32, turned[-1][1], turned[0][3])
            high = jnp.where(lane < 96, turned[-1][3], turned[0][1])
        else:
            q, j = divmod(b - 1, 4)
            x = turned[q]
            if j < 3:
                low, high = x[j], x[(j + 2) % 4]
            else:
                y = turned[q + 1]
                low = jnp.where(lane < 32, x[3], y[3])
                high = jnp.where(lane < 96, x[1], y[1])
        value = jnp.where(lane < 64, low, high)
        s_ref[pl.ds(first * PITCH + b, count, stride=PITCH), :] = value
    for b in range(cols // BLK + 1, PITCH):
        s_ref[pl.ds(first * PITCH + b, count, stride=PITCH), :] = jnp.zeros((count, 128), F32)


def group_rows(s_ref, a_ref, start, end, step):
    first_half = iota((step, 128), 1) < 64
    for m in range(start, end, step):
        for h in range(GROUP // 2):
            even = s_ref[m + 2 * h * PITCH : m + 2 * h * PITCH + step, :]
            odd = s_ref[m + (2 * h + 1) * PITCH : m + (2 * h + 1) * PITCH + step, :]
            a_ref[m : m + step, 128 * h : 128 * h + 128] = jnp.where(first_half, even, odd).astype(BF16)


def correlate(a_ref, starts, count, table_ref):
    fields = None
    for g in range(0, KS, GROUP):
        taken = min(GROUP, KS - g)
        right = table_ref[g : g + taken].reshape(taken * 2 * BLK, 256)
        if taken % 2:
            right = jnp.concatenate([right, jnp.zeros((2 * BLK, 256), BF16)], axis=0)
        lanes = slice(0, right.shape[0])
        parts = [a_ref[m + PITCH * g : m + PITCH * g + count, lanes] for m in starts]
        left = parts[0] if len(parts) == 1 else jnp.concatenate(parts, axis=0)
        term = jnp.dot(left, right, preferred_element_type=F32)
        fields = term if fields is None else fields + term
    return fields


def resist_and_gradient(fields, signed, wv, gs_ref, at):
    weighted = fields * wv
    square = fields * weighted
    intensity = square[:, :128] + square[:, 128:]
    intensity = intensity + pltpu.roll(intensity, 64, 1)
    intensity = intensity + pltpu.roll(intensity, 32, 1)
    resist = 1.0 / (1.0 + jnp.exp(3.0 - intensity))
    miss = resist - jnp.where(signed > 0.0, 1.0, 0.0)
    pull = jnp.abs(signed) * miss
    slope = 4.0 * pull * (resist * (1.0 - resist))
    for h in range(2):
        lanes = slice(128 * h, 128 * h + 128)
        gs_ref[at : at + fields.shape[0], lanes] = (weighted[:, lanes] * slope).astype(gs_ref.dtype)
    return miss, pull


def imaging_kernel(
    inbox_ref, table_ref, signed_ref, left_ref, right_ref, inside_ref, wv_ref,
    loss_ref, edges_ref, gs_ref, mask_ref, s_ref, a_ref, sw_ref,
):
    rows, cols = signed_ref.shape
    halo = 2 * RAD
    tall = rows + 2 * halo
    words = [inbox_ref[:, 0, :].T, inbox_ref[:, 1, :].T]
    lower = [(x & 0xFFFF).astype(F32) * 0.25 for x in words]
    upper = [(x >> 16).astype(F32) * 0.25 for x in words]
    cell = iota((BLK, 128), 0).astype(F32).astype(BF16)
    cell_end = (iota((BLK, 128), 0) + 1).astype(F32).astype(BF16)

    def covers(group, at, first, count):
        low8, high8 = lower[group][at : at + CAP, :], upper[group][at : at + CAP, :]
        stacked = []
        for base in range(first, first + count, BLK):
            low = jnp.clip(low8 - float(base), 0.0, float(BLK))
            high = jnp.clip(high8 - float(base), 0.0, float(BLK))
            parts = []
            for rank in range(CAP):
                lo = jnp.broadcast_to(low[rank : rank + 1, :], (BLK, 128)).astype(BF16)
                hi = jnp.broadcast_to(high[rank : rank + 1, :], (BLK, 128)).astype(BF16)
                parts.append(jnp.maximum(jnp.minimum(hi, cell_end) - jnp.maximum(lo, cell), 0.0))
            stacked.append(jnp.concatenate(parts, axis=1))
        return stacked[0] if len(stacked) == 1 else jnp.concatenate(stacked, axis=0)

    row_span = {-1: (rows - halo, halo, 0), 0: (0, rows, halo), 1: (0, halo, halo + rows)}
    col_span = {-1: (cols - halo, halo, cols + halo), 0: (0, cols, 0), 1: (0, halo, cols)}
    for n, (dr, dc) in enumerate(NEIGHBOURS + [(0, 0)]):
        group, at = (1, 0) if n == 8 else (0, 16 * n)
        r_first, r_count, r_at = row_span[dr]
        c_first, c_count, c_at = col_span[dc]
        row_cover = covers(group, at + 8, r_first, r_count)
        col_cover = covers(group, at, c_first, c_count)
        part = dot_nt(row_cover, col_cover).astype(BF16).astype(F32)
        mask_ref[r_at : r_at + r_count, c_at : c_at + c_count] = part

    edges_ref[0:64, :] = mask_ref[0:64, :].astype(BF16)
    edges_ref[64:112, :] = mask_ref[tall - 48 : tall, :].astype(BF16)
    windows(mask_ref[RAD : tall - RAD + 8, :], s_ref, RAD, cols)
    group_rows(s_ref, a_ref, RAD * PITCH, (tall - RAD) * PITCH, 16 * PITCH)
    left = jnp.where(inside_ref[2:3, 0:1] > 0.0, left_ref[...], 0.0)
    right = jnp.where(inside_ref[3:4, 0:1] > 0.0, right_ref[...], 0.0)
    spread(signed_ref, left, right, sw_ref, rows, cols)

    wv = wv_ref[...]
    chunk = rows // 8 * PITCH
    block = iota((chunk, 128), 0) % PITCH
    co = iota((chunk, 128), 1) & (BLK - 1)
    own = ((block > 0) | (co >= RAD)) & ((block < cols // BLK) | (co < RAD)) & (block <= cols // BLK)
    total = jnp.zeros((1, 128), F32)
    ahead = correlate(a_ref, [RAD * PITCH], chunk, table_ref)
    for k in range(8):
        m = k * chunk
        fields = ahead
        if k < 7:
            ahead = correlate(a_ref, [RAD * PITCH + m + chunk], chunk, table_ref)
        signed = sw_ref[m : m + chunk, :]
        miss, pull = resist_and_gradient(fields, signed, wv, gs_ref, m)
        part = jnp.where(own, pull * miss, 0.0)
        total = total + jnp.sum(part, axis=0, keepdims=True)
    total = 0.25 * jnp.sum(total, axis=1, keepdims=True)
    loss_ref[...] = jnp.broadcast_to(total, loss_ref.shape)


def imaging(inbox, table, signed, left, right, inside, wv, devices):
    rows, cols = signed.shape
    tall = rows + 4 * RAD
    return pl.pallas_call(
        imaging_kernel,
        out_shape=(
            pltpu.VMEM((devices, 1, 128), F32),
            pltpu.VMEM((112, cols + 128), BF16),
            pltpu.VMEM((rows * PITCH, 256), BF16),
        ),
        in_specs=[WHOLE] * 7,
        scratch_shapes=[
            pltpu.VMEM((tall, cols + 128), F32),
            pltpu.VMEM(((tall + 8) * PITCH, 128), F32),
            pltpu.VMEM((tall * PITCH, 64 * GROUP), BF16),
            pltpu.VMEM((rows * PITCH, 128), F32),
        ],
        compiler_params=pltpu.CompilerParams(vmem_limit_bytes=VMEM_LIMIT),
        cost_estimate=pl.CostEstimate(flops=4 * 10**9, bytes_accessed=8 * 10**6, transcendentals=10**6),
    )(inbox, table, signed, left, right, inside, wv)


def adjoint_taps(table_ref, start, at):
    first, last = max(start, 0), min(start + 8, KS)
    pieces = [table_ref[first:last, at : at + BLK, :].reshape((last - first) * BLK, 256)]
    if first > start:
        pieces.insert(0, jnp.zeros(((first - start) * BLK, 256), BF16))
    if last < start + 8:
        pieces.append(jnp.zeros(((start + 8 - last) * BLK, 256), BF16))
    return pieces[0] if len(pieces) == 1 else jnp.concatenate(pieces, axis=0)


def adjoint_kernel(
    edges_ref, table_ref, gs_ref, top_ref, bottom_ref, inside_ref, wv_ref,
    out_ref, s_ref, a_ref, x_ref, sw_ref, gw_ref, g_ref, acc_ref, tile_ref,
):
    rows, cols = out_ref.shape
    ext = rows + 2 * RAD
    x_ref[0:RAD, :] = jnp.where(inside_ref[0:1, 0:1] > 0.0, top_ref[...], 0.0)
    x_ref[RAD : 2 * RAD, :] = jnp.where(inside_ref[1:2, 0:1] > 0.0, bottom_ref[...], 0.0)
    left = jnp.where(inside_ref[2:3, 0:1] > 0.0, x_ref[:, cols + RAD : cols + 2 * RAD], 0.0)
    right = jnp.where(inside_ref[3:4, 0:1] > 0.0, x_ref[:, cols : cols + RAD], 0.0)
    spread(x_ref, left, right, sw_ref, 2 * RAD, cols)
    s_ref[112 * PITCH :, :] = jnp.zeros((8 * PITCH, 128), F32)
    windows(edges_ref[0:64, :].astype(F32), s_ref, 0, cols)
    windows(edges_ref[64:112, :].astype(F32), s_ref, 64, cols)
    group_rows(s_ref, a_ref, 0, 48 * PITCH, 16 * PITCH)
    group_rows(s_ref, a_ref, 64 * PITCH, 112 * PITCH, 16 * PITCH)
    fields = correlate(a_ref, [0, 64 * PITCH], RAD * PITCH, table_ref)
    resist_and_gradient(fields, sw_ref[...], wv_ref[...], gw_ref, 0)
    gw_ref[2 * RAD * PITCH :, :] = gs_ref[...].astype(F32)

    for r in range(ext):
        for s in range(2):
            if r < RAD:
                row = r
            elif r >= RAD + rows:
                row = r - rows
            else:
                row = r + RAD
            at = row * PITCH + s
            g_ref[s, r % 8, r // 8] = gw_ref[at : at + 16, :].astype(BF16)

    total = jnp.zeros((256, 256), F32)
    for i in range(40):
        for s in range(2):
            fields = g_ref[s, i % 8, i // 8 : i // 8 + 16].reshape(256, 256)
            total = total + dot_nt(fields, adjoint_taps(table_ref, KS - 1 - i, BLK * (1 - s)))
    for h in range(2):
        acc_ref[h] = total[:, 128 * h : 128 * h + 128]
    for q in range(cols // 128):
        for h in range(2):
            per_block = [acc_ref[h, pl.ds(4 * q + j, 16, stride=16), :] for j in range(4)]
            for j in range(4):
                pieces = [x[:, BLK * j : BLK * j + BLK] for x in per_block]
                tile_ref[q, pl.ds(4 * h + j, 16, stride=8), :] = jnp.concatenate(pieces, axis=1)
        out_ref[:, 128 * q : 128 * q + 128] = tile_ref[q]


def adjoint(edges, table, gs, top, bottom, inside, wv, rows, cols):
    ext = rows + 2 * RAD
    return pl.pallas_call(
        adjoint_kernel,
        out_shape=jax.ShapeDtypeStruct((rows, cols), F32),
        in_specs=[WHOLE] * 7,
        scratch_shapes=[
            pltpu.VMEM((120 * PITCH, 128), F32),
            pltpu.VMEM((112 * PITCH, 64 * GROUP), BF16),
            pltpu.VMEM((2 * RAD, cols + 2 * RAD), F32),
            pltpu.VMEM((2 * RAD * PITCH, 128), F32),
            pltpu.VMEM((ext * PITCH, 256), F32),
            pltpu.VMEM((2, 8, ext // 8, 16, 256), BF16),
            pltpu.VMEM((2, 256, 128), F32),
            pltpu.VMEM((cols // 128, rows, 128), F32),
        ],
        compiler_params=pltpu.CompilerParams(vmem_limit_bytes=VMEM_LIMIT),
        cost_estimate=pl.CostEstimate(flops=4 * 10**9, bytes_accessed=10**7, transcendentals=0),
    )(edges, table, gs, top, bottom, inside, wv)


def shards(rects, owner, counts, target, loss_weight, kernel, socs_weight):
    row_devices = lax.axis_size("row")
    col_devices = lax.axis_size("col")
    devices = row_devices * col_devices
    rows, cols = target.shape
    outbox, signed, *strips, by_row = make_outbox(
        rects, owner, counts, target, loss_weight, kernel.transpose(1, 0, 2), devices, col_devices
    )
    inbox = lax.all_to_all(outbox, ("row", "col"), split_axis=0, concat_axis=0, tiled=True)
    table = make_tables(by_row)
    top, bottom, left, right, inside = weight_strips(*strips)
    wv = jnp.repeat(socs_weight, 2 * BLK).reshape(1, kernel.shape[0] * BLK)
    local, edges, gs = imaging(inbox, table, signed, left, right, inside, wv, devices)
    losses = lax.all_to_all(local, ("row", "col"), split_axis=0, concat_axis=0, tiled=True)
    mask_grad = adjoint(edges, table, gs, top, bottom, inside, wv, rows, cols)
    window_area = rows * row_devices * cols * col_devices
    return (mask_grad, (jnp.sum(losses[:, 0, 0]) / window_area).reshape(1))


def solution(mesh):
    placed = (
        P(None, ("row", "col")),
        P(("row", "col")),
        P(("row", "col")),
        P("row", "col"),
        P("row", "col"),
        P(),
        P(),
    )
    return jax.shard_map(
        shards, mesh=mesh, in_specs=placed, out_specs=(P("row", "col"), P()), check_vma=False
    )
```

```python
import jax
import jax.numpy as jnp
from jax import lax
from jax.experimental import pallas as pl
from jax.experimental.pallas import tpu as pltpu
from jax.sharding import PartitionSpec as P

RAD = 16
CAP = 8
KS = 33
BLK = 32
GROUP = 8
WIDE = 2 * BLK + 1
PITCH = 18
NEIGHBOURS = [(dr, dc) for dr in (-1, 0, 1) for dc in (-1, 0, 1) if (dr, dc) != (0, 0)]
F32 = jnp.float32
BF16 = jnp.bfloat16
VMEM_LIMIT = 32 * 1024 * 1024


def dot_nt(a, b):
    return lax.dot_general(a, b, (((1,), (1,)), ((), ())), preferred_element_type=F32)


def iota(shape, dim):
    return lax.broadcasted_iota(jnp.int32, shape, dim)


def outbox_kernel(
    tile_cols, counts_ref, rects_ref, owner_ref, target_ref, weight_ref, kernel_ref,
    out_ref, signed_ref, top_ref, bottom_ref, left_ref, right_ref, kernel_out_ref,
    pad_ref, box_ref, target_buf, weight_buf, sems,
):
    rows, cols = signed_ref.shape
    load_target = pltpu.make_async_copy(target_ref, target_buf, sems.at[0])
    load_weight = pltpu.make_async_copy(weight_ref, weight_buf, sems.at[1])
    load_target.start()
    load_weight.start()
    load_kernel = pltpu.make_async_copy(kernel_ref, kernel_out_ref, sems.at[3])
    load_kernel.start()
    slots = owner_ref.shape[1]
    tiles = out_ref.shape[0]
    live = iota((1, slots), 1) < counts_ref[0]
    own = jnp.where(live, owner_ref[...], -1)
    hit = iota((tiles, slots), 0) == own
    hits = jnp.where(hit, 1.0, 0.0).astype(BF16)
    before = jnp.where(iota((slots, slots), 0) < iota((slots, slots), 1), 1.0, 0.0).astype(BF16)
    earlier = jnp.dot(hits, before, preferred_element_type=F32)
    rank = jnp.sum(jnp.where(hit, earlier, 0.0), axis=0, keepdims=True).astype(jnp.int32)
    row = iota((16, slots), 0)
    chosen = rank == (row & 7)
    vertical = (row & 8) == 8

    def placed(first, second):
        value = jnp.where(vertical, second, first)
        value = jnp.where(chosen, value, 0)
        high = (value >> 4).astype(F32).astype(BF16)
        low = (value & 15).astype(F32).astype(BF16)
        return (16.0 * dot_nt(hits, high) + dot_nt(hits, low)).astype(jnp.int32)

    lower = placed(rects_ref[0:1, :], rects_ref[2:3, :])
    upper = placed(rects_ref[1:2, :], rects_ref[3:4, :])
    word = lower + (upper << 16)
    word = jnp.concatenate([word] * 8, axis=1)
    pad_ref[...] = jnp.zeros(pad_ref.shape, jnp.int32)
    pad_ref[24 : 24 + tiles, :] = word
    column = iota((tiles, 128), 0) % tile_cols
    group = iota((tiles, 128), 1) >> 4
    result = jnp.zeros((tiles, 128), jnp.int32)
    for n, (dr, dc) in enumerate(NEIGHBOURS):
        start = 24 + dr * tile_cols + dc
        inside = (column + dc >= 0) & (column + dc < tile_cols) & (group == n)
        result = jnp.where(inside, pad_ref[start : start + tiles, :], result)
    box_ref[:, 0, :] = result
    box_ref[:, 1, :] = word
    store = pltpu.make_async_copy(box_ref, out_ref, sems.at[2])
    store.start()
    load_target.wait()
    load_weight.wait()
    signed_ref[...] = jnp.where(target_buf[...] > 0, weight_buf[...], -weight_buf[...])
    top_ref[...] = signed_ref[0:RAD, :]
    bottom_ref[...] = signed_ref[rows - RAD : rows, :]
    left_ref[...] = signed_ref[:, 0:RAD]
    right_ref[...] = signed_ref[:, cols - RAD : cols]
    load_kernel.wait()
    store.wait()


SMALL = pl.BlockSpec(memory_space=pltpu.SMEM)
WHOLE = pl.BlockSpec(memory_space=pltpu.VMEM)
ANYWHERE = pl.BlockSpec(memory_space=pl.ANY)


def make_outbox(rects, owner, counts, target, weight, kernel, tiles, tile_cols):
    slots = owner.shape[0]
    rows, cols = target.shape
    return pl.pallas_call(
        lambda *refs: outbox_kernel(tile_cols, *refs),
        out_shape=(
            jax.ShapeDtypeStruct((tiles, 2, 128), jnp.int32),
            pltpu.VMEM((rows, cols), F32),
            pltpu.VMEM((RAD, cols), F32),
            pltpu.VMEM((RAD, cols), F32),
            pltpu.VMEM((rows, RAD), F32),
            pltpu.VMEM((rows, RAD), F32),
            pltpu.VMEM(kernel.shape, BF16),
        ),
        in_specs=[SMALL, WHOLE, WHOLE, ANYWHERE, ANYWHERE, ANYWHERE],
        out_specs=(ANYWHERE,) + (WHOLE,) * 6,
        scratch_shapes=[
            pltpu.VMEM((tiles + 48, 128), jnp.int32),
            pltpu.VMEM((tiles, 2, 128), jnp.int32),
            pltpu.VMEM((rows, cols), jnp.int32),
            pltpu.VMEM((rows, cols), F32),
            pltpu.SemaphoreType.DMA((4,)),
        ],
        cost_estimate=pl.CostEstimate(flops=10**8, bytes_accessed=10**6, transcendentals=0),
    )(counts, rects, owner.reshape(1, slots), target, weight, kernel)


def tables_kernel(kernel_ref, table_ref, wide_ref):
    channels = kernel_ref.shape[1]
    lanes = channels * BLK
    tap, lane = iota((KS, lanes), 0), iota((KS, lanes), 1) % BLK
    flat = kernel_ref[...].astype(F32).reshape(KS * channels, KS).astype(BF16)
    mine = iota((KS, channels, lanes), 1) == iota((KS, channels, lanes), 2) // BLK

    def by_lane(picked):
        every = jnp.dot(flat, jnp.where(picked, 1.0, 0.0).astype(BF16), preferred_element_type=F32)
        return jnp.sum(jnp.where(mine, every.reshape(KS, channels, lanes), 0.0), axis=1)

    taps = by_lane(tap == KS - 1 - lane)
    edge = by_lane(tap == 0)
    co = iota((KS, 128), 1) % BLK
    for p in range(BLK):
        for h in range(lanes // 128):
            mine = taps[:, 128 * h : 128 * h + 128]
            ends = edge[:, 128 * h : 128 * h + 128]
            near = pltpu.roll(mine, p, 1) if p else mine
            far = pltpu.roll(mine, p + 128 - BLK, 1)
            far = jnp.where(co < p, far, jnp.where(co == p, ends, 0.0))
            wide_ref[h, pl.ds(p, KS, stride=WIDE), :] = far
            wide_ref[h, pl.ds(BLK + p, KS, stride=WIDE), :] = jnp.where(co >= p, near, 0.0)
    for a in range(KS):
        for h in range(lanes // 128):
            table_ref[a, :, 128 * h : 128 * h + 128] = wide_ref[h, a * WIDE : a * WIDE + 2 * BLK, :].astype(BF16)


def make_tables(kernel):
    lanes = kernel.shape[1] * BLK
    return pl.pallas_call(
        tables_kernel,
        out_shape=pltpu.VMEM((KS, 2 * BLK, lanes), BF16),
        in_specs=[WHOLE],
        scratch_shapes=[pltpu.VMEM((lanes // 128, KS * WIDE + 8, 128), F32)],
        compiler_params=pltpu.CompilerParams(vmem_limit_bytes=VMEM_LIMIT // 2),
        cost_estimate=pl.CostEstimate(flops=10**10, bytes_accessed=10**6, transcendentals=0),
    )(kernel)


def weight_strips(top_rows, bottom_rows, left_cols, right_cols):
    def beside(first, last, axis):
        count = lax.axis_size(axis)
        up = [(i, (i + 1) % count) for i in range(count)]
        down = [(j, i) for i, j in up]
        return lax.ppermute(last, axis, up), lax.ppermute(first, axis, down)

    c = lax.axis_index("col")
    left_cols = jnp.where(c > 0, left_cols, 0.0)
    right_cols = jnp.where(c < lax.axis_size("col") - 1, right_cols, 0.0)
    left, right = beside(left_cols, right_cols, "col")
    last = right.shape[0] - RAD
    top, bottom = beside(
        jnp.concatenate([top_rows, right[:RAD], left[:RAD]], axis=1),
        jnp.concatenate([bottom_rows, right[last:], left[last:]], axis=1),
        "row",
    )
    r, c = lax.axis_index("row"), lax.axis_index("col")
    inside = jnp.stack([r > 0, r < lax.axis_size("row") - 1, c > 0, c < lax.axis_size("col") - 1])
    return top, bottom, left, right, jnp.broadcast_to(inside.astype(F32)[:, None], (4, 128))


def spread(x_ref, left, right, out_ref, rows, cols):
    for b in range(cols // BLK + 1):
        if b == 0:
            piece = jnp.concatenate([left, x_ref[:, 0:RAD]], axis=1)
        elif b == cols // BLK:
            piece = jnp.concatenate([x_ref[:, cols - RAD : cols], right], axis=1)
        else:
            piece = x_ref[:, BLK * b - RAD : BLK * b + RAD]
        out_ref[pl.ds(b, rows, stride=PITCH), :] = jnp.concatenate([piece] * 4, axis=1)
    for b in range(cols // BLK + 1, PITCH):
        out_ref[pl.ds(b, rows, stride=PITCH), :] = jnp.zeros((rows, 128), F32)


def windows(mask, s_ref, first, cols):
    count = mask.shape[0]
    lane = iota((count, 128), 1)
    tiles = [mask[:, 128 * q : 128 * q + 128] for q in range(cols // 128 + 1)]
    turned = [[x] + [pltpu.roll(x, 128 - BLK * j, 1) for j in (1, 2, 3)] for x in tiles]
    for b in range(cols // BLK + 1):
        if b == 0:
            low = jnp.where(lane < 32, turned[-1][1], turned[0][3])
            high = jnp.where(lane < 96, turned[-1][3], turned[0][1])
        else:
            q, j = divmod(b - 1, 4)
            x = turned[q]
            if j < 3:
                low, high = x[j], x[(j + 2) % 4]
            else:
                y = turned[q + 1]
                low = jnp.where(lane < 32, x[3], y[3])
                high = jnp.where(lane < 96, x[1], y[1])
        value = jnp.where(lane < 64, low, high)
        s_ref[pl.ds(first * PITCH + b, count, stride=PITCH), :] = value
    for b in range(cols // BLK + 1, PITCH):
        s_ref[pl.ds(first * PITCH + b, count, stride=PITCH), :] = jnp.zeros((count, 128), F32)


def group_rows(s_ref, a_ref, start, end, step):
    first_half = iota((step, 128), 1) < 64
    for m in range(start, end, step):
        for h in range(GROUP // 2):
            even = s_ref[m + 2 * h * PITCH : m + 2 * h * PITCH + step, :]
            odd = s_ref[m + (2 * h + 1) * PITCH : m + (2 * h + 1) * PITCH + step, :]
            a_ref[m : m + step, 128 * h : 128 * h + 128] = jnp.where(first_half, even, odd).astype(BF16)


def correlate(a_ref, starts, count, table_ref):
    fields = None
    for g in range(0, KS, GROUP):
        taken = min(GROUP, KS - g)
        right = table_ref[g : g + taken].reshape(taken * 2 * BLK, 256)
        if taken % 2:
            right = jnp.concatenate([right, jnp.zeros((2 * BLK, 256), BF16)], axis=0)
        lanes = slice(0, right.shape[0])
        parts = [a_ref[m + PITCH * g : m + PITCH * g + count, lanes] for m in starts]
        left = parts[0] if len(parts) == 1 else jnp.concatenate(parts, axis=0)
        term = jnp.dot(left, right, preferred_element_type=F32)
        fields = term if fields is None else fields + term
    return fields


def resist_and_gradient(fields, signed, wv, gs_ref, at):
    weighted = fields * wv
    square = fields * weighted
    intensity = square[:, :128] + square[:, 128:]
    intensity = intensity + pltpu.roll(intensity, 64, 1)
    intensity = intensity + pltpu.roll(intensity, 32, 1)
    resist = 1.0 / (1.0 + jnp.exp(3.0 - intensity))
    miss = resist - jnp.where(signed > 0.0, 1.0, 0.0)
    pull = jnp.abs(signed) * miss
    slope = 4.0 * pull * (resist * (1.0 - resist))
    for h in range(2):
        lanes = slice(128 * h, 128 * h + 128)
        gs_ref[at : at + fields.shape[0], lanes] = (weighted[:, lanes] * slope).astype(gs_ref.dtype)
    return miss, pull


def imaging_kernel(
    inbox_ref, table_ref, signed_ref, left_ref, right_ref, wv_ref,
    loss_ref, edges_ref, gs_ref, mask_ref, s_ref, a_ref, sw_ref,
):
    rows, cols = signed_ref.shape
    halo = 2 * RAD
    tall = rows + 2 * halo
    words = [inbox_ref[:, 0, :].T, inbox_ref[:, 1, :].T]
    lower = [(x & 0xFFFF).astype(F32) * 0.25 for x in words]
    upper = [(x >> 16).astype(F32) * 0.25 for x in words]
    cell = iota((BLK, 128), 0).astype(F32).astype(BF16)
    cell_end = (iota((BLK, 128), 0) + 1).astype(F32).astype(BF16)

    def covers(group, at, first, count):
        low8, high8 = lower[group][at : at + CAP, :], upper[group][at : at + CAP, :]
        stacked = []
        for base in range(first, first + count, BLK):
            low = jnp.clip(low8 - float(base), 0.0, float(BLK))
            high = jnp.clip(high8 - float(base), 0.0, float(BLK))
            parts = []
            for rank in range(CAP):
                lo = jnp.broadcast_to(low[rank : rank + 1, :], (BLK, 128)).astype(BF16)
                hi = jnp.broadcast_to(high[rank : rank + 1, :], (BLK, 128)).astype(BF16)
                parts.append(jnp.maximum(jnp.minimum(hi, cell_end) - jnp.maximum(lo, cell), 0.0))
            stacked.append(jnp.concatenate(parts, axis=1))
        return stacked[0] if len(stacked) == 1 else jnp.concatenate(stacked, axis=0)

    row_span = {-1: (rows - halo, halo, 0), 0: (0, rows, halo), 1: (0, halo, halo + rows)}
    col_span = {-1: (cols - halo, halo, cols + halo), 0: (0, cols, 0), 1: (0, halo, cols)}
    for n, (dr, dc) in enumerate(NEIGHBOURS + [(0, 0)]):
        group, at = (1, 0) if n == 8 else (0, 16 * n)
        r_first, r_count, r_at = row_span[dr]
        c_first, c_count, c_at = col_span[dc]
        row_cover = covers(group, at + 8, r_first, r_count)
        col_cover = covers(group, at, c_first, c_count)
        part = dot_nt(row_cover, col_cover).astype(BF16).astype(F32)
        mask_ref[r_at : r_at + r_count, c_at : c_at + c_count] = part

    edges_ref[0:64, :] = mask_ref[0:64, :].astype(BF16)
    edges_ref[64:112, :] = mask_ref[tall - 48 : tall, :].astype(BF16)
    windows(mask_ref[RAD : tall - RAD + 8, :], s_ref, RAD, cols)
    group_rows(s_ref, a_ref, RAD * PITCH, (tall - RAD) * PITCH, 16 * PITCH)
    spread(signed_ref, left_ref[...], right_ref[...], sw_ref, rows, cols)

    wv = wv_ref[...]
    chunk = rows // 8 * PITCH
    block = iota((chunk, 128), 0) % PITCH
    co = iota((chunk, 128), 1) & (BLK - 1)
    own = ((block > 0) | (co >= RAD)) & ((block < cols // BLK) | (co < RAD)) & (block <= cols // BLK)
    total = jnp.zeros((1, 128), F32)
    ahead = correlate(a_ref, [RAD * PITCH], chunk, table_ref)
    for k in range(8):
        m = k * chunk
        fields = ahead
        if k < 7:
            ahead = correlate(a_ref, [RAD * PITCH + m + chunk], chunk, table_ref)
        signed = sw_ref[m : m + chunk, :]
        miss, pull = resist_and_gradient(fields, signed, wv, gs_ref, m)
        part = jnp.where(own, pull * miss, 0.0)
        total = total + jnp.sum(part, axis=0, keepdims=True)
    total = 0.25 * jnp.sum(total, axis=1, keepdims=True)
    loss_ref[...] = jnp.broadcast_to(total, loss_ref.shape)


def imaging(inbox, table, signed, left, right, wv, devices):
    rows, cols = signed.shape
    tall = rows + 4 * RAD
    return pl.pallas_call(
        imaging_kernel,
        out_shape=(
            pltpu.VMEM((devices, 1, 128), F32),
            pltpu.VMEM((112, cols + 128), BF16),
            pltpu.VMEM((rows * PITCH, 256), BF16),
        ),
        in_specs=[WHOLE] * 6,
        scratch_shapes=[
            pltpu.VMEM((tall, cols + 128), F32),
            pltpu.VMEM(((tall + 8) * PITCH, 128), F32),
            pltpu.VMEM((tall * PITCH, 64 * GROUP), BF16),
            pltpu.VMEM((rows * PITCH, 128), F32),
        ],
        compiler_params=pltpu.CompilerParams(vmem_limit_bytes=VMEM_LIMIT),
        cost_estimate=pl.CostEstimate(flops=4 * 10**9, bytes_accessed=8 * 10**6, transcendentals=10**6),
    )(inbox, table, signed, left, right, wv)


def adjoint_taps(table_ref, start, at):
    first, last = max(start, 0), min(start + 8, KS)
    pieces = [table_ref[first:last, at : at + BLK, :].reshape((last - first) * BLK, 256)]
    if first > start:
        pieces.insert(0, jnp.zeros(((first - start) * BLK, 256), BF16))
    if last < start + 8:
        pieces.append(jnp.zeros(((start + 8 - last) * BLK, 256), BF16))
    return pieces[0] if len(pieces) == 1 else jnp.concatenate(pieces, axis=0)


def adjoint_kernel(
    edges_ref, table_ref, gs_ref, top_ref, bottom_ref, inside_ref, wv_ref,
    out_ref, s_ref, a_ref, x_ref, sw_ref, gw_ref, g_ref, acc_ref, tile_ref,
):
    rows, cols = out_ref.shape
    ext = rows + 2 * RAD
    x_ref[0:RAD, :] = jnp.where(inside_ref[0:1, 0:1] > 0.0, top_ref[...], 0.0)
    x_ref[RAD : 2 * RAD, :] = jnp.where(inside_ref[1:2, 0:1] > 0.0, bottom_ref[...], 0.0)
    left = jnp.where(inside_ref[2:3, 0:1] > 0.0, x_ref[:, cols + RAD : cols + 2 * RAD], 0.0)
    right = jnp.where(inside_ref[3:4, 0:1] > 0.0, x_ref[:, cols : cols + RAD], 0.0)
    spread(x_ref, left, right, sw_ref, 2 * RAD, cols)
    s_ref[112 * PITCH :, :] = jnp.zeros((8 * PITCH, 128), F32)
    windows(edges_ref[0:64, :].astype(F32), s_ref, 0, cols)
    windows(edges_ref[64:112, :].astype(F32), s_ref, 64, cols)
    group_rows(s_ref, a_ref, 0, 48 * PITCH, 16 * PITCH)
    group_rows(s_ref, a_ref, 64 * PITCH, 112 * PITCH, 16 * PITCH)
    fields = correlate(a_ref, [0, 64 * PITCH], RAD * PITCH, table_ref)
    resist_and_gradient(fields, sw_ref[...], wv_ref[...], gw_ref, 0)
    gw_ref[2 * RAD * PITCH :, :] = gs_ref[...].astype(F32)

    for r in range(ext):
        for s in range(2):
            if r < RAD:
                row = r
            elif r >= RAD + rows:
                row = r - rows
            else:
                row = r + RAD
            at = row * PITCH + s
            g_ref[s, r % 8, r // 8] = gw_ref[at : at + 16, :].astype(BF16)

    total = jnp.zeros((256, 256), F32)
    for i in range(40):
        for s in range(2):
            fields = g_ref[s, i % 8, i // 8 : i // 8 + 16].reshape(256, 256)
            total = total + dot_nt(fields, adjoint_taps(table_ref, KS - 1 - i, BLK * (1 - s)))
    for h in range(2):
        acc_ref[h] = total[:, 128 * h : 128 * h + 128]
    for q in range(cols // 128):
        for h in range(2):
            per_block = [acc_ref[h, pl.ds(4 * q + j, 16, stride=16), :] for j in range(4)]
            for j in range(4):
                pieces = [x[:, BLK * j : BLK * j + BLK] for x in per_block]
                tile_ref[q, pl.ds(4 * h + j, 16, stride=8), :] = jnp.concatenate(pieces, axis=1)
        out_ref[:, 128 * q : 128 * q + 128] = tile_ref[q]


def adjoint(edges, table, gs, top, bottom, inside, wv, rows, cols):
    ext = rows + 2 * RAD
    return pl.pallas_call(
        adjoint_kernel,
        out_shape=jax.ShapeDtypeStruct((rows, cols), F32),
        in_specs=[WHOLE] * 7,
        scratch_shapes=[
            pltpu.VMEM((120 * PITCH, 128), F32),
            pltpu.VMEM((112 * PITCH, 64 * GROUP), BF16),
            pltpu.VMEM((2 * RAD, cols + 2 * RAD), F32),
            pltpu.VMEM((2 * RAD * PITCH, 128), F32),
            pltpu.VMEM((ext * PITCH, 256), F32),
            pltpu.VMEM((2, 8, ext // 8, 16, 256), BF16),
            pltpu.VMEM((2, 256, 128), F32),
            pltpu.VMEM((cols // 128, rows, 128), F32),
        ],
        compiler_params=pltpu.CompilerParams(vmem_limit_bytes=VMEM_LIMIT),
        cost_estimate=pl.CostEstimate(flops=4 * 10**9, bytes_accessed=10**7, transcendentals=0),
    )(edges, table, gs, top, bottom, inside, wv)


def shards(rects, owner, counts, target, loss_weight, kernel, socs_weight):
    row_devices = lax.axis_size("row")
    col_devices = lax.axis_size("col")
    devices = row_devices * col_devices
    rows, cols = target.shape
    outbox, signed, *strips, by_row = make_outbox(
        rects, owner, counts, target, loss_weight, kernel.transpose(1, 0, 2), devices, col_devices
    )
    inbox = lax.all_to_all(outbox, ("row", "col"), split_axis=0, concat_axis=0, tiled=True)
    table = make_tables(by_row)
    top, bottom, left, right, inside = weight_strips(*strips)
    wv = jnp.repeat(socs_weight, 2 * BLK).reshape(1, kernel.shape[0] * BLK)
    local, edges, gs = imaging(inbox, table, signed, left, right, wv, devices)
    losses = lax.all_to_all(local, ("row", "col"), split_axis=0, concat_axis=0, tiled=True)
    mask_grad = adjoint(edges, table, gs, top, bottom, inside, wv, rows, cols)
    window_area = rows * row_devices * cols * col_devices
    return (mask_grad, (jnp.sum(losses[:, 0, 0]) / window_area).reshape(1))


def solution(mesh):
    placed = (
        P(None, ("row", "col")),
        P(("row", "col")),
        P(("row", "col")),
        P("row", "col"),
        P("row", "col"),
        P(),
        P(),
    )
    return jax.shard_map(
        shards, mesh=mesh, in_specs=placed, out_specs=(P("row", "col"), P()), check_vma=False
    )
```
